32 devices in a mesh: parts: 2 (over y), row: 4 (over z), frame: 4 (over x, core).
Axes of the slice: x: 2, y: 2, z: 4, core: 2. Of those that a mesh axis runs over, the one named last changes fastest.
Arguments:
- latent: bfloat16 [8, 8, 16, 512], P(('parts', 'frame'), 'row'), parts along dimension 0, may hold values from -15 to 15
- qkv_weight: bfloat16 [3, 512, 512], P(None, 'frame'), may hold values from -0.125 to 0.125
- out_weight: bfloat16 [512, 512], P('frame'), may hold values from -0.25 to 0.25
- attn_gain: float32 [512], replicated, may hold values from 0.1 to 1.9
- in_weight: bfloat16 [512, 2, 2048], P(None, None, 'frame'), may hold values from -0.25 to 0.25
- depth_weight: float32 [3, 3, 2, 2048], replicated, may hold values from -2 to 2
- down_weight: bfloat16 [2048, 512], P('frame'), may hold values from -0.125 to 0.125
- mlp_gain: float32 [512], replicated, may hold values from 0.1 to 1.9
- conv_first: bfloat16 [3, 3, 3, 512, 512], P(None, None, None, 'frame'), may hold values from -0.0546875 to 0.0546875
- conv_second: bfloat16 [3, 3, 3, 512, 512], P(None, None, None, 'frame'), may hold values from -0.0546875 to 0.0546875
Outputs:
- decoded: bfloat16 [8, 8, 16, 512], P('parts', 'row', 'frame'), parts along dimension 0
The draws below stay inside these ranges and needn't reach their ends.
There are 2 independent parts, one for each index of `parts`. The reference program is written for one: setup_inputs(seed, part) draws one part's arguments, and reference() takes and returns one part's arrays. A program takes and returns all parts, laid end to end along the dimension named above; an argument that names none is the same for every part. Nothing has to cross between parts.
All inputs are finite; a program needn't handle non-finite values.
Results may differ from the reference program's by a relative error of at most 0.015.
Values may be sent and summed in bfloat16 or wider, within the bound.
No kernel may reach another device: no remote copies, remote signals or barrier semaphores. Data moves between devices by JAX's collectives and lax.ppermute only.
A program may use at most 128 MiB of HBM per device.

```python
import jax
import jax.numpy as jnp
from jax import lax

CH = 512
HEAD = 32
INNER = 2048
COLS = 16
FRAMES = 4
HEIGHT = 8


def draw_latent(key, part):
    shape = (FRAMES, HEIGHT, COLS, CH)
    ramp = 1.0 + 2.0 * jnp.arange(HEIGHT, dtype=jnp.float32) / max(HEIGHT - 1, 1)
    values = jax.random.normal(jax.random.fold_in(key, 7), shape, jnp.float32) * ramp[None, :, None, None]
    return jnp.clip(values, -15.0, 15.0).astype(jnp.bfloat16)


def level_of(stream_key, dims, shards, low, largest):
    factor_of = 1.0
    for axis_at, shards_of in shards:
        draws = jax.random.uniform(jax.random.fold_in(jax.random.fold_in(stream_key, 6), axis_at), (shards_of,), jnp.float32, low / len(shards), largest / len(shards))
        factor_of = factor_of * jnp.repeat(jnp.exp(draws), dims[axis_at] // shards_of).reshape((-1,) + (1,) * (len(dims) - 1 - axis_at))
    return factor_of


def gaussian(own_key, extent, scale, limit, pieces=(), kind=jnp.bfloat16):
    level = level_of(own_key, extent, pieces, -0.22, 0.18) if pieces else 1.0
    result = jax.random.normal(own_key, extent, jnp.float32) * scale * level
    return jnp.minimum(jnp.maximum(result, -limit), limit).astype(kind)


def setup_inputs(seed: int = 0, part: int = 0) -> dict:
    splits = jax.random.split(jax.random.key(seed), 11)
    part_splits = jax.random.split(jax.random.fold_in(splits[10], part), 11)
    return {
        "latent": draw_latent(jax.random.fold_in(jax.random.fold_in(splits[10], part), 71), part),
        "qkv_weight": gaussian(splits[1], (3, CH, CH), (4 * CH) ** -0.5, 0.125, ((1, 4),)),
        "out_weight": gaussian(splits[2], (CH, CH), CH ** -0.5, 0.25, ((0, 4),)),
        "attn_gain": jnp.clip(1.0 + 0.18 * jax.random.normal(splits[3], (CH,), jnp.float32), 0.1, 1.9),
        "in_weight": gaussian(splits[4], (CH, 2, INNER), CH ** -0.5, 0.25, ((2, 4),)),
        "depth_weight": gaussian(splits[5], (3, 3, 2, INNER), 9 ** -0.5, 2.0, (), jnp.float32),
        "down_weight": gaussian(splits[6], (INNER, CH), INNER ** -0.5, 0.125, ((0, 4),)),
        "mlp_gain": jnp.clip(1.0 + 0.18 * jax.random.normal(splits[7], (CH,), jnp.float32), 0.1, 1.9),
        "conv_first": gaussian(splits[8], (3, 3, 3, CH, CH), (27 * CH) ** -0.5, 0.0546875, ((3, 4),)),
        "conv_second": gaussian(splits[9], (3, 3, 3, CH, CH), (27 * CH) ** -0.5, 0.0546875, ((3, 4),)),
    }


def norm_rows(values, gain):
    return values * lax.rsqrt(lax.optimization_barrier(jnp.mean(values * values, axis=-1, keepdims=True)) + 1e-05) * gain

def conv_full(field, kernel):
    kernel_io = jnp.transpose(kernel, (0, 1, 2, 4, 3))
    return lax.conv_general_dilated(field[None].astype(jnp.float32), kernel_io.astype(jnp.float32), (1, 1, 1), ((1, 1), (1, 1), (1, 1)), dimension_numbers=('NDHWC', 'DHWIO', 'NDHWC'), precision=lax.Precision.HIGHEST)[0]

def reference(latent, qkv_weight, out_weight, attn_gain, in_weight, depth_weight, down_weight, mlp_gain, conv_first, conv_second):
    frames, height, columns, width = latent.shape
    heads = width // HEAD
    flat_in = latent.reshape(-1, width)
    packed = jnp.dot(flat_in, qkv_weight.reshape(3 * width, width).T, preferred_element_type=jnp.float32).astype(jnp.bfloat16)
    packed = packed.reshape(frames, height * columns, 3, heads, HEAD)
    query = jnp.maximum(packed[:, :, 0], 0).astype(jnp.float32)
    keys = jnp.maximum(packed[:, :, 1], 0).astype(jnp.float32)
    values = packed[:, :, 2].astype(jnp.float32)
    count = height * columns
    state = jnp.einsum('fnhd,fnhe->fhde', keys, values, precision=lax.Precision.HIGHEST) / count
    key_mean = lax.optimization_barrier(jnp.sum(keys, axis=1)) / count
    numer = jnp.einsum('fnhd,fhde->fnhe', query, state, precision=lax.Precision.HIGHEST)
    denom = jnp.maximum(jnp.einsum('fnhd,fhd->fnh', query, key_mean, precision=lax.Precision.HIGHEST), 1.0)
    mixed = (numer / denom[..., None]).astype(jnp.bfloat16).reshape(-1, width)
    attn_out = jnp.dot(mixed, out_weight, preferred_element_type=jnp.float32)
    first = (flat_in.astype(jnp.float32) + norm_rows(attn_out, attn_gain)).astype(jnp.bfloat16)
    inner = jax.nn.silu(jnp.dot(first, in_weight.reshape(width, -1), preferred_element_type=jnp.float32)).astype(jnp.bfloat16)
    inner = inner.reshape(frames, height, columns, 2, -1)
    padded = jnp.pad(inner, ((0, 0), (1, 1), (1, 1), (0, 0), (0, 0)))
    spread = jnp.zeros(inner.shape, jnp.float32)
    for shift_row in range(3):
        for shift_col in range(3):
            spread = spread + padded[:, shift_row:shift_row + height, shift_col:shift_col + columns].astype(jnp.float32) * depth_weight[shift_row, shift_col]
    gated = (spread[..., 0, :] * jax.nn.silu(spread[..., 1, :])).astype(jnp.bfloat16)
    mlp_out = jnp.dot(gated.reshape(frames * height * columns, -1), down_weight, preferred_element_type=jnp.float32)
    second = (first.astype(jnp.float32) + norm_rows(mlp_out, mlp_gain)).astype(jnp.bfloat16)
    second = second.reshape(frames, height, columns, width)
    hidden_conv = jax.nn.silu(conv_full(second, conv_first)).astype(jnp.bfloat16)
    return (second.astype(jnp.float32) + conv_full(hidden_conv, conv_second)).astype(jnp.bfloat16)
```

```python
import jax
import jax.numpy as jnp
from jax import lax
from jax.sharding import PartitionSpec as P

HEAD = 32


def padded_2(cells, sides, width):
    for axis, dim in sides:
        count = lax.axis_size(axis)
        ends = count - 1
        head = lax.slice_in_dim(cells, 0, width, axis=dim)
        tail = lax.slice_in_dim(cells, cells.shape[dim] - width, cells.shape[dim], axis=dim)
        cells = jnp.concatenate(
            [
                lax.ppermute(tail, axis, [(i, (i + 1) % count) for i in range(ends)]),
                cells,
                lax.ppermute(head, axis, [((i + 1) % count, i) for i in range(ends)]),
            ],
            axis=dim,
        )
    return cells


def norm_rows(values, gain):
    return values * lax.rsqrt(jnp.mean(values * values, axis=-1, keepdims=True) + 1e-05) * gain


def attend(packed):
    frames, height, columns = (packed.shape[0], packed.shape[1], packed.shape[2])
    width = packed.shape[4]
    heads = width // HEAD
    flat = packed.reshape(frames, height * columns, 3, heads, HEAD)
    query = jnp.maximum(flat[:, :, 0], 0)
    keys = jnp.maximum(flat[:, :, 1], 0)
    values = flat[:, :, 2]
    state = jnp.einsum("fnhd,fnhe->fhde", keys, values, preferred_element_type=jnp.float32)
    key_total = jnp.sum(keys.astype(jnp.float32), axis=1)
    state, key_total = (
        lax.psum(state.astype(jnp.bfloat16), "row").astype(jnp.float32),
        lax.psum(key_total.astype(jnp.bfloat16), "row").astype(jnp.float32),
    )
    count = height * lax.axis_size("row") * columns
    state = state / count
    key_mean = key_total / count
    query_wide = query.astype(jnp.float32)
    numer = jnp.einsum("fnhd,fhde->fnhe", query_wide, state, precision=lax.Precision.HIGHEST)
    denom = jnp.maximum(
        jnp.einsum("fnhd,fhd->fnh", query_wide, key_mean, precision=lax.Precision.HIGHEST), 1.0
    )
    return (numer / denom[..., None]).astype(jnp.bfloat16).reshape(frames, height, columns, width)


def depth_mix(inner, depth_local):
    height, columns = (inner.shape[1], inner.shape[2])
    extended = padded_2(inner, (("row", 1),), 1)
    padded = jnp.pad(extended, ((0, 0), (0, 0), (1, 1), (0, 0), (0, 0)))
    spread = jnp.zeros(inner.shape, jnp.float32)
    for shift_row in range(3):
        for shift_col in range(3):
            spread = (
                spread
                + padded[:, shift_row : shift_row + height, shift_col : shift_col + columns].astype(
                    jnp.float32
                )
                * depth_local[shift_row, shift_col]
            )
    return (spread[..., 0, :] * jax.nn.silu(spread[..., 1, :])).astype(jnp.bfloat16)


def conv_tile(extended, kernel):
    frames, padded_rows, columns, width = extended.shape
    height = padded_rows - 2
    out_width = kernel.shape[3]
    padded = jnp.pad(extended, ((1, 1), (0, 0), (1, 1), (0, 0)))
    result = jnp.zeros((frames * height * columns, out_width), jnp.float32)
    for shift_time in range(3):
        for shift_row in range(3):
            slab = padded[shift_time : shift_time + frames, shift_row : shift_row + height]
            stacked = jnp.stack(
                [slab[:, :, shift_col : shift_col + columns] for shift_col in range(3)], axis=3
            )
            result = result + jnp.einsum(
                "nci,coi->no",
                stacked.reshape(-1, 3, width),
                kernel[shift_time, shift_row],
                preferred_element_type=jnp.float32,
            )
    return result.reshape(frames, height, columns, out_width)


def local(
    latent,
    qkv_weight,
    out_weight,
    attn_gain,
    in_weight,
    depth_weight,
    down_weight,
    mlp_gain,
    conv_first,
    conv_second,
):
    frames, height, columns, width = latent.shape
    place = lax.axis_index("frame")
    packed = jnp.einsum(
        "frwc,kjc->frwkj",
        latent,
        lax.all_gather(qkv_weight, "frame", axis=1, tiled=True),
        preferred_element_type=jnp.float32,
    ).astype(jnp.bfloat16)
    mixed = attend(packed)
    section = mixed
    attn_out = jnp.einsum(
        "frwj,jc->frwc",
        section,
        lax.all_gather(out_weight, "frame", axis=0, tiled=True),
        preferred_element_type=jnp.float32,
    )
    first = (latent.astype(jnp.float32) + norm_rows(attn_out, attn_gain)).astype(jnp.bfloat16)
    inner = jax.nn.silu(
        jnp.einsum(
            "frwc,ckj->frwkj",
            first,
            lax.all_gather(in_weight, "frame", axis=2, tiled=True),
            preferred_element_type=jnp.float32,
        )
    ).astype(jnp.bfloat16)
    gated = depth_mix(inner, depth_weight)
    section = gated
    mlp_out = jnp.einsum(
        "frwj,jc->frwc",
        section,
        lax.all_gather(down_weight, "frame", axis=0, tiled=True),
        preferred_element_type=jnp.float32,
    )
    second = (first.astype(jnp.float32) + norm_rows(mlp_out, mlp_gain)).astype(jnp.bfloat16)
    gathered = lax.all_gather(second, "frame", axis=0, tiled=True)
    out_share = conv_first.shape[3]
    extended = padded_2(gathered, (("row", 1),), 2)
    activated = jax.nn.silu(conv_tile(extended, conv_first))
    global_row = lax.axis_index("row") * height - 1 + lax.iota(jnp.int32, height + 2)
    inside = ((global_row >= 0) & (global_row < height * lax.axis_size("row"))).astype(jnp.float32)
    hidden_conv = (activated * inside[None, :, None, None]).astype(jnp.bfloat16)
    joined = lax.all_gather(hidden_conv, "frame", axis=3, tiled=True)
    result = conv_tile(joined, conv_second)
    own_part = lax.dynamic_slice_in_dim(gathered, place * out_share, out_share, 3)
    final = (own_part.astype(jnp.float32) + result).astype(jnp.bfloat16)
    return lax.all_to_all(final, "frame", split_axis=2, concat_axis=3, tiled=True)


def swap(cells, mask):
    count = lax.axis_size("frame")
    return lax.ppermute(cells, "frame", [(i, i ^ mask) for i in range(count)])


def in_order(pieces, place, dim):
    step = 1
    while step < len(pieces):
        flip = (place & step) != 0
        pieces = [
            jnp.where(flip, pieces[i ^ step], pieces[i]) for i in range(len(pieces))
        ]
        step *= 2
    return jnp.concatenate(pieces, axis=dim)


def gathered_by_mask(cells):
    count = lax.axis_size("frame")
    pieces = [None] * count
    pieces[0] = cells
    masks = list(range(3, count, 2))
    for mask in masks:
        pieces[mask] = swap(cells, mask)
    both = swap(jnp.stack([pieces[m] for m in [0] + masks]), 1)
    for i, mask in enumerate([0] + masks):
        pieces[mask ^ 1] = both[i]
    return pieces


def silu(values):
    return values / (1.0 + jnp.exp(-values))


def by_frames(
    latent,
    qkv_weight,
    out_weight,
    attn_gain,
    in_weight,
    depth_weight,
    down_weight,
    mlp_gain,
    conv_first,
    conv_second,
):
    count = lax.axis_size("frame")
    level, place = (lax.axis_index("row"), lax.axis_index("frame"))
    rows, columns, width = latent.shape[1:]
    height = rows * count
    tokens = height * columns
    share = qkv_weight.shape[1]
    own = latent.reshape(rows * columns, width)
    pieces = [None] * count
    masks = [1] + list(range(2, count, 2))
    for mask in masks:
        pairs = [
            (z * count + f, f * count + (z ^ mask)) for z in range(count) for f in range(count)
        ]
        pieces[mask] = lax.ppermute(own, ("row", "frame"), pairs)
    both = swap(jnp.stack([pieces[m] for m in masks]), 1)
    for i, mask in enumerate(masks):
        pieces[mask ^ 1] = both[i]
    cells = in_order(pieces, place, 0)
    out_pieces = gathered_by_mask(out_weight)
    packed = jnp.einsum(
        "tc,kjc->tkj", cells, qkv_weight, preferred_element_type=jnp.float32
    ).astype(jnp.bfloat16)
    query = jnp.maximum(packed[:, 0], 0)
    keys = jnp.maximum(packed[:, 1], 0)
    values = packed[:, 2]
    head_of = lax.iota(jnp.int32, share) // HEAD
    same = head_of[:, None] == head_of[None, :]
    state = jnp.einsum("td,te->de", keys, values, preferred_element_type=jnp.float32) / tokens
    key_mean = jnp.sum(keys.astype(jnp.float32), axis=0) / tokens
    table = jnp.concatenate(
        [jnp.where(same, state, 0.0), jnp.where(same, key_mean[:, None], 0.0)], axis=1
    )
    both = jnp.einsum("td,de->te", query.astype(jnp.float32), table, precision=lax.Precision.HIGHEST)
    mixed = (both[:, :share] / jnp.maximum(both[:, share:], 1.0)).astype(jnp.bfloat16)
    mixed_pieces = gathered_by_mask(mixed)
    attn_out = sum(
        jnp.dot(a, b, preferred_element_type=jnp.float32)
        for a, b in zip(mixed_pieces, out_pieces)
    )
    first = (cells.astype(jnp.float32) + norm_rows(attn_out, attn_gain)).astype(jnp.bfloat16)
    units = in_weight.shape[2]
    inner = silu(
        jnp.einsum("tc,ckj->tkj", first, in_weight, preferred_element_type=jnp.float32)
    ).astype(jnp.bfloat16)
    taps = lax.dynamic_slice_in_dim(depth_weight, place * units, units, 3)
    padded = jnp.pad(
        inner.reshape(height, columns, 2, units), ((1, 1), (1, 1), (0, 0), (0, 0))
    ).astype(jnp.float32)
    spread = sum(
        padded[i : i + height, j : j + columns] * taps[i, j] for i in range(3) for j in range(3)
    )
    gated = (spread[:, :, 0] * silu(spread[:, :, 1])).astype(jnp.bfloat16)
    partial = jnp.einsum(
        "rwj,jc->rwc", gated, down_weight, preferred_element_type=jnp.float32
    )
    half = columns // 2
    mine = (place ^ (place >> 1)) & 1
    kept = lax.dynamic_slice_in_dim(partial, mine * half, half, 1)
    sent = lax.dynamic_slice_in_dim(partial, (1 - mine) * half, half, 1)
    total = kept + swap(sent, 1)
    far = [swap(total.astype(jnp.bfloat16), mask).astype(jnp.float32) for mask in range(3, count, 2)]
    mlp_out = total + sum(far)
    first_half = lax.dynamic_slice_in_dim(
        first.reshape(height, columns, width), mine * half, half, 1
    )
    second = (first_half.astype(jnp.float32) + norm_rows(mlp_out, mlp_gain)).astype(jnp.bfloat16)
    framed = jnp.pad(second, ((2, 2), (0, 0), (0, 0)))
    parts = []
    for mask in range(count):
        piece = lax.dynamic_slice_in_dim(framed, (level ^ mask) * rows, rows + 4, 0)
        if mask:
            piece = lax.ppermute(piece, "row", [(i, i ^ mask) for i in range(count)])
        parts.append(piece[None])
    window = in_order(parts, level, 0)
    other = swap(window, 1)
    lead = jnp.where(mine == 0, window, other)
    tail = jnp.where(mine == 0, other, window)
    window = jnp.concatenate([lead, tail], axis=2)
    activated = silu(conv_tile(window, conv_first))
    global_row = level * rows - 1 + lax.iota(jnp.int32, rows + 2)
    inside = ((global_row >= 0) & (global_row < height)).astype(jnp.float32)
    hidden = (activated * inside[None, :, None, None]).astype(jnp.bfloat16)
    joined = in_order(gathered_by_mask(hidden), place, 3)
    result = conv_tile(joined, conv_second)
    own_part = lax.dynamic_slice_in_dim(window[:, 2 : 2 + rows], place * share, share, 3)
    final = (own_part.astype(jnp.float32) + result).astype(jnp.bfloat16)
    strip = columns // count
    def strip_of(mask):
        return lax.dynamic_slice_in_dim(final, (place ^ mask) * strip, strip, 2)
    outs = [strip_of(0)] + [swap(strip_of(mask), mask) for mask in range(1, count)]
    return in_order(outs, place, 3)


def solution(mesh):
    body = by_frames if mesh.shape["row"] == mesh.shape["frame"] else local
    in_specs = (
        P(("parts", "frame"), "row", None, None),
        P(None, "frame", None),
        P("frame", None),
        P(),
        P(None, None, "frame"),
        P(),
        P("frame", None),
        P(),
        P(None, None, None, "frame", None),
        P(None, None, None, "frame", None),
    )
    out_specs = P("parts", "row", "frame", None)
    return jax.shard_map(body, mesh=mesh, in_specs=in_specs, out_specs=out_specs, check_vma=False)
```

```python
import functools

import jax
import jax.numpy as jnp
from jax import lax
from jax.experimental import pallas as pl
from jax.experimental.pallas import tpu as pltpu
from jax.sharding import PartitionSpec as P

HEAD = 32


def padded_2(cells, sides, width):
    for axis, dim in sides:
        count = lax.axis_size(axis)
        ends = count - 1
        head = lax.slice_in_dim(cells, 0, width, axis=dim)
        tail = lax.slice_in_dim(cells, cells.shape[dim] - width, cells.shape[dim], axis=dim)
        cells = jnp.concatenate(
            [
                lax.ppermute(tail, axis, [(i, (i + 1) % count) for i in range(ends)]),
                cells,
                lax.ppermute(head, axis, [((i + 1) % count, i) for i in range(ends)]),
            ],
            axis=dim,
        )
    return cells


def norm_rows(values, gain):
    return values * lax.rsqrt(jnp.mean(values * values, axis=-1, keepdims=True) + 1e-05) * gain


def attend(packed):
    frames, height, columns = (packed.shape[0], packed.shape[1], packed.shape[2])
    width = packed.shape[4]
    heads = width // HEAD
    flat = packed.reshape(frames, height * columns, 3, heads, HEAD)
    query = jnp.maximum(flat[:, :, 0], 0)
    keys = jnp.maximum(flat[:, :, 1], 0)
    values = flat[:, :, 2]
    state = jnp.einsum("fnhd,fnhe->fhde", keys, values, preferred_element_type=jnp.float32)
    key_total = jnp.sum(keys.astype(jnp.float32), axis=1)
    state, key_total = (
        lax.psum(state.astype(jnp.bfloat16), "row").astype(jnp.float32),
        lax.psum(key_total.astype(jnp.bfloat16), "row").astype(jnp.float32),
    )
    count = height * lax.axis_size("row") * columns
    state = state / count
    key_mean = key_total / count
    query_wide = query.astype(jnp.float32)
    numer = jnp.einsum("fnhd,fhde->fnhe", query_wide, state, precision=lax.Precision.HIGHEST)
    denom = jnp.maximum(
        jnp.einsum("fnhd,fhd->fnh", query_wide, key_mean, precision=lax.Precision.HIGHEST), 1.0
    )
    return (numer / denom[..., None]).astype(jnp.bfloat16).reshape(frames, height, columns, width)


def depth_mix(inner, depth_local):
    height, columns = (inner.shape[1], inner.shape[2])
    extended = padded_2(inner, (("row", 1),), 1)
    padded = jnp.pad(extended, ((0, 0), (0, 0), (1, 1), (0, 0), (0, 0)))
    spread = jnp.zeros(inner.shape, jnp.float32)
    for shift_row in range(3):
        for shift_col in range(3):
            spread = (
                spread
                + padded[:, shift_row : shift_row + height, shift_col : shift_col + columns].astype(
                    jnp.float32
                )
                * depth_local[shift_row, shift_col]
            )
    return (spread[..., 0, :] * jax.nn.silu(spread[..., 1, :])).astype(jnp.bfloat16)


def conv_tile(extended, kernel):
    frames, padded_rows, columns, width = extended.shape
    height = padded_rows - 2
    out_width = kernel.shape[3]
    padded = jnp.pad(extended, ((1, 1), (0, 0), (1, 1), (0, 0)))
    result = jnp.zeros((frames * height * columns, out_width), jnp.float32)
    for shift_time in range(3):
        for shift_row in range(3):
            slab = padded[shift_time : shift_time + frames, shift_row : shift_row + height]
            stacked = jnp.stack(
                [slab[:, :, shift_col : shift_col + columns] for shift_col in range(3)], axis=3
            )
            result = result + jnp.einsum(
                "nci,coi->no",
                stacked.reshape(-1, 3, width),
                kernel[shift_time, shift_row],
                preferred_element_type=jnp.float32,
            )
    return result.reshape(frames, height, columns, out_width)


def local(
    latent,
    qkv_weight,
    out_weight,
    attn_gain,
    in_weight,
    depth_weight,
    down_weight,
    mlp_gain,
    conv_first,
    conv_second,
):
    frames, height, columns, width = latent.shape
    place = lax.axis_index("frame")
    packed = jnp.einsum(
        "frwc,kjc->frwkj",
        latent,
        lax.all_gather(qkv_weight, "frame", axis=1, tiled=True),
        preferred_element_type=jnp.float32,
    ).astype(jnp.bfloat16)
    mixed = attend(packed)
    section = mixed
    attn_out = jnp.einsum(
        "frwj,jc->frwc",
        section,
        lax.all_gather(out_weight, "frame", axis=0, tiled=True),
        preferred_element_type=jnp.float32,
    )
    first = (latent.astype(jnp.float32) + norm_rows(attn_out, attn_gain)).astype(jnp.bfloat16)
    inner = jax.nn.silu(
        jnp.einsum(
            "frwc,ckj->frwkj",
            first,
            lax.all_gather(in_weight, "frame", axis=2, tiled=True),
            preferred_element_type=jnp.float32,
        )
    ).astype(jnp.bfloat16)
    gated = depth_mix(inner, depth_weight)
    section = gated
    mlp_out = jnp.einsum(
        "frwj,jc->frwc",
        section,
        lax.all_gather(down_weight, "frame", axis=0, tiled=True),
        preferred_element_type=jnp.float32,
    )
    second = (first.astype(jnp.float32) + norm_rows(mlp_out, mlp_gain)).astype(jnp.bfloat16)
    gathered = lax.all_gather(second, "frame", axis=0, tiled=True)
    out_share = conv_first.shape[3]
    extended = padded_2(gathered, (("row", 1),), 2)
    activated = jax.nn.silu(conv_tile(extended, conv_first))
    global_row = lax.axis_index("row") * height - 1 + lax.iota(jnp.int32, height + 2)
    inside = ((global_row >= 0) & (global_row < height * lax.axis_size("row"))).astype(jnp.float32)
    hidden_conv = (activated * inside[None, :, None, None]).astype(jnp.bfloat16)
    joined = lax.all_gather(hidden_conv, "frame", axis=3, tiled=True)
    result = conv_tile(joined, conv_second)
    own_part = lax.dynamic_slice_in_dim(gathered, place * out_share, out_share, 3)
    final = (own_part.astype(jnp.float32) + result).astype(jnp.bfloat16)
    return lax.all_to_all(final, "frame", split_axis=2, concat_axis=3, tiled=True)


def swap(cells, mask):
    count = lax.axis_size("frame")
    return lax.ppermute(cells, "frame", [(i, i ^ mask) for i in range(count)])


def in_order(pieces, place, dim):
    step = 1
    while step < len(pieces):
        flip = (place & step) != 0
        pieces = [jnp.where(flip, pieces[i ^ step], pieces[i]) for i in range(len(pieces))]
        step *= 2
    return jnp.concatenate(pieces, axis=dim)


def gathered_by_mask(cells):
    count = lax.axis_size("frame")
    pieces = [None] * count
    pieces[0] = cells
    masks = list(range(3, count, 2))
    for mask in masks:
        pieces[mask] = swap(cells, mask)
    for mask in [0] + masks:
        pieces[mask ^ 1] = swap(pieces[mask], 1)
    return pieces


def silu(values):
    return values / (1.0 + jnp.exp(-values))


def half_of(place):
    return (place ^ (place >> 1)) & 1


def call(body, operands, outs, scratch=(), flops=0):
    moved = sum(o.size * o.dtype.itemsize for o in operands)
    return pl.pallas_call(
        body,
        out_shape=[jax.ShapeDtypeStruct(shape, kind) for shape, kind in outs],
        scratch_shapes=[pltpu.VMEM(shape, kind) for shape, kind in scratch],
        compiler_params=pltpu.CompilerParams(vmem_limit_bytes=40 * 1024 * 1024),
        cost_estimate=pl.CostEstimate(flops=flops, bytes_accessed=moved, transcendentals=0),
    )(*operands)


def attend_body(count, *refs):
    pieces, (weight, mixed_ref, cells_ref) = refs[:count], refs[count:]
    place = lax.axis_index("frame")
    rows = pieces[0].shape[0]
    for mask, piece in enumerate(pieces):
        at = pl.multiple_of((place ^ mask) * rows, rows)
        cells_ref[pl.ds(at, rows)] = piece[...]
    tokens, share = mixed_ref.shape
    packed = lax.dot_general(
        cells_ref[...],
        weight[...].reshape(3 * share, weight.shape[2]),
        (((1,), (1,)), ((), ())),
        preferred_element_type=jnp.float32,
    ).astype(jnp.bfloat16)
    query = jnp.maximum(packed[:, :share], 0)
    keys = jnp.maximum(packed[:, share : 2 * share], 0)
    values = packed[:, 2 * share :]
    joined = jnp.concatenate([values, jnp.ones_like(values)], axis=1)
    table = lax.dot_general(
        keys, joined, (((0,), (0,)), ((), ())), preferred_element_type=jnp.float32
    ) * (1.0 / tokens)
    head_in = lax.broadcasted_iota(jnp.int32, table.shape, 0) // HEAD
    head_out = lax.rem(lax.broadcasted_iota(jnp.int32, table.shape, 1), share) // HEAD
    table = jnp.where(head_in == head_out, table, 0.0)
    high = table.astype(jnp.bfloat16)
    low = (table - high.astype(jnp.float32)).astype(jnp.bfloat16)
    both = jnp.dot(query, high, preferred_element_type=jnp.float32) + jnp.dot(
        query, low, preferred_element_type=jnp.float32
    )
    mixed_ref[...] = (both[:, :share] / jnp.maximum(both[:, share:], 1.0)).astype(jnp.bfloat16)


def mlp_body(count, columns, *refs):
    mixed, out_weight = refs[:count], refs[count : 2 * count]
    cells, gain, in_weight, depth, down, kept_ref, sent_ref, first_ref, field = refs[2 * count :]
    place = lax.axis_index("frame")
    tokens, width = cells.shape
    units = down.shape[0]
    height = tokens // columns
    attn_out = sum(
        jnp.dot(a[...], b[...], preferred_element_type=jnp.float32)
        for a, b in zip(mixed, out_weight)
    )
    first = (cells[...].astype(jnp.float32) + norm_rows(attn_out, gain[...])).astype(jnp.bfloat16)
    at = pl.multiple_of(place * units, units)
    column = lax.rem(lax.broadcasted_iota(jnp.int32, (tokens, units), 0), columns)
    blank = jnp.zeros((columns, units), jnp.float32)
    spread = []
    for part in range(2):
        inner = silu(jnp.dot(first, in_weight[part], preferred_element_type=jnp.float32))
        field[pl.ds(0, columns)] = blank
        field[pl.ds(columns, tokens)] = inner.astype(jnp.bfloat16).astype(jnp.float32)
        field[pl.ds(columns + tokens, columns)] = blank
        sides = []
        for shift_col in range(3):
            sides.append(
                sum(
                    field[pl.ds(shift_row * columns, tokens)]
                    * depth[shift_row, shift_col, part : part + 1, pl.ds(at, units)]
                    for shift_row in range(3)
                )
            )
        spread.append(
            jnp.where(column > 0, pltpu.roll(sides[0], 1, 0), 0.0)
            + sides[1]
            + jnp.where(column < columns - 1, pltpu.roll(sides[2], tokens - 1, 0), 0.0)
        )
    gated = (spread[0] * silu(spread[1])).astype(jnp.bfloat16)
    partial = jnp.dot(gated, down[...], preferred_element_type=jnp.float32)
    partial = partial.reshape(height // 2, 2, columns, width)
    first = first.reshape(height // 2, 2, columns, width)
    odd = half_of(place) == 1
    kept_ref[...] = jnp.where(odd, partial[:, 1], partial[:, 0])
    sent_ref[...] = jnp.where(odd, partial[:, 0], partial[:, 1])
    first_ref[...] = jnp.where(odd, first[:, 1], first[:, 0])


def norm_body(far_count, step, *refs):
    total, first, gain = refs[:3]
    far, outs, framed = refs[3 : 3 + far_count], refs[3 + far_count : -1], refs[-1]
    level = lax.axis_index("row")
    mlp_out = total[...]
    for piece in far:
        mlp_out = mlp_out + piece[...].astype(jnp.float32)
    second = first[...].astype(jnp.float32) + norm_rows(mlp_out, gain[...].reshape(1, 1, -1))
    rows = second.shape[0]
    blank = jnp.zeros(framed.shape[1:], framed.dtype)
    framed[0] = blank
    framed[rows + 1] = blank
    framed[1 : rows + 1] = second.astype(jnp.bfloat16)
    for mask, out in enumerate(outs):
        out[...] = framed[pl.ds((level ^ mask) * step, step + 2)]


def conv_rows(field, kernel):
    frames, rows = field.shape[0] - 2, field.shape[1] - 2
    columns, width = field.shape[2:]
    share = kernel.shape[3]
    tokens = frames * rows * columns
    total = None
    for shift_time in range(3):
        for shift_row in range(3):
            slab = field[shift_time : shift_time + frames, shift_row : shift_row + rows]
            term = lax.dot_general(
                slab.reshape(tokens, width),
                kernel[shift_time, shift_row].reshape(3 * share, width),
                (((1,), (1,)), ((), ())),
                preferred_element_type=jnp.float32,
            )
            total = term if total is None else total + term
    column = lax.rem(lax.broadcasted_iota(jnp.int32, (tokens, share), 0), columns)
    before = jnp.where(column > 0, pltpu.roll(total[:, :share], 1, 0), 0.0)
    after = jnp.where(column < columns - 1, pltpu.roll(total[:, 2 * share :], tokens - 1, 0), 0.0)
    return (before + total[:, share : 2 * share] + after).reshape(frames, rows, columns, share)


def clear_ends(field):
    edge = jnp.zeros(field.shape[1:], field.dtype)
    field[0] = edge
    field[field.shape[0] - 1] = edge


def first_conv_body(height, *refs):
    kernel, hidden_ref, part_ref, field = refs[-4:]
    pieces = refs[:-4]
    count = len(pieces) // 2
    level, place = lax.axis_index("row"), lax.axis_index("frame")
    clear_ends(field)
    for index, piece in enumerate(pieces):
        frame = (level ^ (index % count)) + 1
        parity = half_of(place) ^ (index // count)
        for row in range(piece.shape[0]):
            field[frame, 2 * row + parity] = piece[row]
    activated = silu(conv_rows(field, kernel))
    frames, band, columns, share = hidden_ref.shape
    rows = band - 2
    global_row = level * rows - 1 + lax.broadcasted_iota(jnp.int32, activated.shape, 1)
    inside = (global_row >= 0) & (global_row < height)
    hidden_ref[...] = jnp.where(inside, activated, 0.0).astype(jnp.bfloat16)
    at = pl.multiple_of(place * share, share)
    part_ref[...] = field[1 : frames + 1, 2 : 2 + rows, :, pl.ds(at, share)]


def second_conv_body(*refs):
    part, kernel, out_ref, field = refs[-4:]
    pieces = refs[:-4]
    place = lax.axis_index("frame")
    clear_ends(field)
    share = part.shape[3]
    frames = part.shape[0]
    for mask, piece in enumerate(pieces):
        at = pl.multiple_of((place ^ mask) * share, share)
        field[1 : frames + 1, :, :, pl.ds(at, share)] = piece[...]
    result = conv_rows(field, kernel)
    out_ref[...] = (part[...].astype(jnp.float32) + result).astype(jnp.bfloat16)


def by_frames(
    latent,
    qkv_weight,
    out_weight,
    attn_gain,
    in_weight,
    depth_weight,
    down_weight,
    mlp_gain,
    conv_first,
    conv_second,
):
    count = lax.axis_size("frame")
    place = lax.axis_index("frame")
    rows, columns, width = latent.shape[1:]
    height = rows * count
    tokens = height * columns
    share = qkv_weight.shape[1]
    units = down_weight.shape[0]
    half = height // 2
    bf16, f32 = jnp.bfloat16, jnp.float32
    own = latent.reshape(rows * columns, width)
    pieces = [None] * count
    masks = [1] + list(range(2, count, 2))
    for mask in masks:
        pairs = [
            (z * count + f, f * count + (z ^ mask)) for z in range(count) for f in range(count)
        ]
        pieces[mask] = lax.ppermute(own, ("row", "frame"), pairs)
    for mask in masks:
        pieces[mask ^ 1] = swap(pieces[mask], 1)
    out_pieces = gathered_by_mask(out_weight)
    in_parts = jnp.transpose(in_weight, (1, 0, 2))
    mixed, cells = call(
        functools.partial(attend_body, count),
        [*pieces, qkv_weight],
        [((tokens, share), bf16), ((tokens, width), bf16)],
        flops=2 * tokens * width * 3 * share,
    )
    kept, sent, first = call(
        functools.partial(mlp_body, count, columns),
        [
            *gathered_by_mask(mixed),
            *out_pieces,
            cells,
            attn_gain.reshape(1, width),
            in_parts,
            depth_weight,
            down_weight,
        ],
        [((half, columns, width), f32)] * 2 + [((half, columns, width), bf16)],
        scratch=[((tokens + 2 * columns, units), f32)],
        flops=2 * tokens * width * (width + 3 * units),
    )
    total = kept + swap(sent, 1)
    far = [swap(total.astype(bf16), mask) for mask in range(3, count, 2)]
    step = rows // 2
    windows = call(
        functools.partial(norm_body, len(far), step),
        [total, first, mlp_gain.reshape(1, width), *far],
        [((step + 2, columns, width), bf16)] * count,
        scratch=[((half + 2, columns, width), bf16)],
        flops=8 * total.size,
    )
    windows = list(windows)
    for mask in range(1, count):
        windows[mask] = lax.ppermute(windows[mask], "row", [(i, i ^ mask) for i in range(count)])
    others = [swap(window, 1) for window in windows]
    hidden, own_part = call(
        functools.partial(first_conv_body, height),
        [*windows, *others, conv_first],
        [((count, rows + 2, columns, share), bf16), ((count, rows, columns, share), bf16)],
        scratch=[((count + 2, rows + 4, columns, width), bf16)],
        flops=2 * count * (rows + 2) * columns * 27 * width * share,
    )
    (final,) = call(
        second_conv_body,
        [*gathered_by_mask(hidden), own_part, conv_second],
        [((count, rows, columns, share), bf16)],
        scratch=[((count + 2, rows + 2, columns, width), bf16)],
        flops=2 * count * rows * columns * 27 * width * share,
    )
    strip = columns // count
    strips = [
        lax.dynamic_slice_in_dim(final, (place ^ mask) * strip, strip, 2) for mask in range(count)
    ]
    outs = [strips[0]] + [swap(strips[mask], mask) for mask in range(1, count)]
    return in_order(outs, place, 3)


def solution(mesh):
    body = by_frames if mesh.shape["row"] == mesh.shape["frame"] else local
    in_specs = (
        P(("parts", "frame"), "row", None, None),
        P(None, "frame", None),
        P("frame", None),
        P(),
        P(None, None, "frame"),
        P(),
        P("frame", None),
        P(),
        P(None, None, None, "frame", None),
        P(None, None, None, "frame", None),
    )
    out_specs = P("parts", "row", "frame", None)
    return jax.shard_map(body, mesh=mesh, in_specs=in_specs, out_specs=out_specs, check_vma=False)
```

```python
import functools

import jax
import jax.numpy as jnp
from jax import lax
from jax.experimental import pallas as pl
from jax.experimental.pallas import tpu as pltpu
from jax.sharding import PartitionSpec as P

HEAD = 32


def padded_2(cells, sides, width):
    for axis, dim in sides:
        count = lax.axis_size(axis)
        ends = count - 1
        head = lax.slice_in_dim(cells, 0, width, axis=dim)
        tail = lax.slice_in_dim(cells, cells.shape[dim] - width, cells.shape[dim], axis=dim)
        cells = jnp.concatenate(
            [
                lax.ppermute(tail, axis, [(i, (i + 1) % count) for i in range(ends)]),
                cells,
                lax.ppermute(head, axis, [((i + 1) % count, i) for i in range(ends)]),
            ],
            axis=dim,
        )
    return cells


def norm_rows(values, gain):
    return values * lax.rsqrt(jnp.mean(values * values, axis=-1, keepdims=True) + 1e-05) * gain


def attend(packed):
    frames, height, columns = (packed.shape[0], packed.shape[1], packed.shape[2])
    width = packed.shape[4]
    heads = width // HEAD
    flat = packed.reshape(frames, height * columns, 3, heads, HEAD)
    query = jnp.maximum(flat[:, :, 0], 0)
    keys = jnp.maximum(flat[:, :, 1], 0)
    values = flat[:, :, 2]
    state = jnp.einsum("fnhd,fnhe->fhde", keys, values, preferred_element_type=jnp.float32)
    key_total = jnp.sum(keys.astype(jnp.float32), axis=1)
    state, key_total = (
        lax.psum(state.astype(jnp.bfloat16), "row").astype(jnp.float32),
        lax.psum(key_total.astype(jnp.bfloat16), "row").astype(jnp.float32),
    )
    count = height * lax.axis_size("row") * columns
    state = state / count
    key_mean = key_total / count
    query_wide = query.astype(jnp.float32)
    numer = jnp.einsum("fnhd,fhde->fnhe", query_wide, state, precision=lax.Precision.HIGHEST)
    denom = jnp.maximum(
        jnp.einsum("fnhd,fhd->fnh", query_wide, key_mean, precision=lax.Precision.HIGHEST), 1.0
    )
    return (numer / denom[..., None]).astype(jnp.bfloat16).reshape(frames, height, columns, width)


def depth_mix(inner, depth_local):
    height, columns = (inner.shape[1], inner.shape[2])
    extended = padded_2(inner, (("row", 1),), 1)
    padded = jnp.pad(extended, ((0, 0), (0, 0), (1, 1), (0, 0), (0, 0)))
    spread = jnp.zeros(inner.shape, jnp.float32)
    for shift_row in range(3):
        for shift_col in range(3):
            spread = (
                spread
                + padded[:, shift_row : shift_row + height, shift_col : shift_col + columns].astype(
                    jnp.float32
                )
                * depth_local[shift_row, shift_col]
            )
    return (spread[..., 0, :] * jax.nn.silu(spread[..., 1, :])).astype(jnp.bfloat16)


def conv_tile(extended, kernel):
    frames, padded_rows, columns, width = extended.shape
    height = padded_rows - 2
    out_width = kernel.shape[3]
    padded = jnp.pad(extended, ((1, 1), (0, 0), (1, 1), (0, 0)))
    result = jnp.zeros((frames * height * columns, out_width), jnp.float32)
    for shift_time in range(3):
        for shift_row in range(3):
            slab = padded[shift_time : shift_time + frames, shift_row : shift_row + height]
            stacked = jnp.stack(
                [slab[:, :, shift_col : shift_col + columns] for shift_col in range(3)], axis=3
            )
            result = result + jnp.einsum(
                "nci,coi->no",
                stacked.reshape(-1, 3, width),
                kernel[shift_time, shift_row],
                preferred_element_type=jnp.float32,
            )
    return result.reshape(frames, height, columns, out_width)


def local(
    latent,
    qkv_weight,
    out_weight,
    attn_gain,
    in_weight,
    depth_weight,
    down_weight,
    mlp_gain,
    conv_first,
    conv_second,
):
    frames, height, columns, width = latent.shape
    place = lax.axis_index("frame")
    packed = jnp.einsum(
        "frwc,kjc->frwkj",
        latent,
        lax.all_gather(qkv_weight, "frame", axis=1, tiled=True),
        preferred_element_type=jnp.float32,
    ).astype(jnp.bfloat16)
    mixed = attend(packed)
    section = mixed
    attn_out = jnp.einsum(
        "frwj,jc->frwc",
        section,
        lax.all_gather(out_weight, "frame", axis=0, tiled=True),
        preferred_element_type=jnp.float32,
    )
    first = (latent.astype(jnp.float32) + norm_rows(attn_out, attn_gain)).astype(jnp.bfloat16)
    inner = jax.nn.silu(
        jnp.einsum(
            "frwc,ckj->frwkj",
            first,
            lax.all_gather(in_weight, "frame", axis=2, tiled=True),
            preferred_element_type=jnp.float32,
        )
    ).astype(jnp.bfloat16)
    gated = depth_mix(inner, depth_weight)
    section = gated
    mlp_out = jnp.einsum(
        "frwj,jc->frwc",
        section,
        lax.all_gather(down_weight, "frame", axis=0, tiled=True),
        preferred_element_type=jnp.float32,
    )
    second = (first.astype(jnp.float32) + norm_rows(mlp_out, mlp_gain)).astype(jnp.bfloat16)
    gathered = lax.all_gather(second, "frame", axis=0, tiled=True)
    out_share = conv_first.shape[3]
    extended = padded_2(gathered, (("row", 1),), 2)
    activated = jax.nn.silu(conv_tile(extended, conv_first))
    global_row = lax.axis_index("row") * height - 1 + lax.iota(jnp.int32, height + 2)
    inside = ((global_row >= 0) & (global_row < height * lax.axis_size("row"))).astype(jnp.float32)
    hidden_conv = (activated * inside[None, :, None, None]).astype(jnp.bfloat16)
    joined = lax.all_gather(hidden_conv, "frame", axis=3, tiled=True)
    result = conv_tile(joined, conv_second)
    own_part = lax.dynamic_slice_in_dim(gathered, place * out_share, out_share, 3)
    final = (own_part.astype(jnp.float32) + result).astype(jnp.bfloat16)
    return lax.all_to_all(final, "frame", split_axis=2, concat_axis=3, tiled=True)


def swap(cells, mask):
    count = lax.axis_size("frame")
    return lax.ppermute(cells, "frame", [(i, i ^ mask) for i in range(count)])


def in_order(pieces, place, dim):
    step = 1
    while step < len(pieces):
        flip = (place & step) != 0
        pieces = [jnp.where(flip, pieces[i ^ step], pieces[i]) for i in range(len(pieces))]
        step *= 2
    return jnp.concatenate(pieces, axis=dim)


def gathered_by_mask(cells):
    count = lax.axis_size("frame")
    pieces = [None] * count
    pieces[0] = cells
    masks = list(range(3, count, 2))
    for mask in masks:
        pieces[mask] = swap(cells, mask)
    for mask in [0] + masks:
        pieces[mask ^ 1] = swap(pieces[mask], 1)
    return pieces


def silu(values):
    return values / (1.0 + jnp.exp(-values))


def half_of(place):
    return (place ^ (place >> 1)) & 1


def call(body, operands, outs, scratch=(), flops=0, room=4):
    moved = sum(o.size * o.dtype.itemsize for o in operands)
    return pl.pallas_call(
        body,
        out_shape=[jax.ShapeDtypeStruct(shape, kind) for shape, kind in outs],
        scratch_shapes=[pltpu.VMEM(shape, kind) for shape, kind in scratch],
        compiler_params=pltpu.CompilerParams(vmem_limit_bytes=room * 1024 * 1024),
        cost_estimate=pl.CostEstimate(flops=flops, bytes_accessed=moved, transcendentals=0),
    )(*operands)


def attend_body(count, *refs):
    pieces, (weight, mixed_ref, cells_ref) = refs[:count], refs[count:]
    place = lax.axis_index("frame")
    rows = pieces[0].shape[0]
    for mask, piece in enumerate(pieces):
        at = pl.multiple_of((place ^ mask) * rows, rows)
        cells_ref[pl.ds(at, rows)] = piece[...]
    tokens, share = mixed_ref.shape
    packed = lax.dot_general(
        cells_ref[...],
        weight[pl.ds(0, 3 * share)],
        (((1,), (1,)), ((), ())),
        preferred_element_type=jnp.float32,
    ).astype(jnp.bfloat16)
    query = jnp.maximum(packed[:, :share], 0)
    keys = jnp.maximum(packed[:, share : 2 * share], 0)
    values = packed[:, 2 * share :]
    joined = jnp.concatenate([values, jnp.ones_like(values)], axis=1)
    table = lax.dot_general(
        keys, joined, (((0,), (0,)), ((), ())), preferred_element_type=jnp.float32
    ) * (1.0 / tokens)
    head_in = lax.broadcasted_iota(jnp.int32, table.shape, 0) // HEAD
    head_out = lax.rem(lax.broadcasted_iota(jnp.int32, table.shape, 1), share) // HEAD
    table = jnp.where(head_in == head_out, table, 0.0)
    high = table.astype(jnp.bfloat16)
    low = (table - high.astype(jnp.float32)).astype(jnp.bfloat16)
    both = jnp.dot(query, high, preferred_element_type=jnp.float32) + jnp.dot(
        query, low, preferred_element_type=jnp.float32
    )
    mixed_ref[...] = (both[:, :share] / jnp.maximum(both[:, share:], 1.0)).astype(jnp.bfloat16)


def mlp_body(count, columns, *refs):
    mixed, out_weight = refs[:count], refs[count : 2 * count - 1]
    cells, weights, scales, kept_ref, sent_ref, first_ref, field = refs[2 * count - 1 :]
    place = lax.axis_index("frame")
    tokens, width = cells.shape
    units = field.shape[1]
    share = mixed[0].shape[1]
    starts = [3 * share, 4 * share, 4 * share + units, 4 * share + units + width]
    own_out, down = weights[pl.ds(starts[0], share)], weights[pl.ds(starts[1], units)]
    height = tokens // columns
    attn_out = sum(
        jnp.dot(a[...], b, preferred_element_type=jnp.float32)
        for a, b in zip(mixed, [own_out] + [piece[...] for piece in out_weight])
    )
    first = (cells[...].astype(jnp.float32) + norm_rows(attn_out, scales[18:19])).astype(jnp.bfloat16)
    column = lax.rem(lax.broadcasted_iota(jnp.int32, (tokens, units), 0), columns)
    blank = jnp.zeros((columns, units), jnp.float32)
    spread = []
    for part in range(2):
        inner = silu(jnp.dot(first, weights[pl.ds(starts[2 + part], width)], preferred_element_type=jnp.float32))
        field[pl.ds(0, columns)] = blank
        field[pl.ds(columns, tokens)] = inner.astype(jnp.bfloat16).astype(jnp.float32)
        field[pl.ds(columns + tokens, columns)] = blank
        sides = []
        for shift_col in range(3):
            sides.append(
                sum(
                    field[pl.ds(shift_row * columns, tokens)]
                    * scales[tap : tap + 1]
                    for shift_row, tap in enumerate(range(2 * shift_col + part, 18, 6))
                )
            )
        spread.append(
            jnp.where(column > 0, pltpu.roll(sides[0], 1, 0), 0.0)
            + sides[1]
            + jnp.where(column < columns - 1, pltpu.roll(sides[2], tokens - 1, 0), 0.0)
        )
    gated = (spread[0] * silu(spread[1])).astype(jnp.bfloat16)
    partial = jnp.dot(gated, down, preferred_element_type=jnp.float32)
    partial = partial.reshape(height // 2, 2, columns, width)
    first = first.reshape(height // 2, 2, columns, width)
    odd = half_of(place) == 1
    kept_ref[...] = jnp.where(odd, partial[:, 1], partial[:, 0])
    sent_ref[...] = jnp.where(odd, partial[:, 0], partial[:, 1])
    first_ref[...] = jnp.where(odd, first[:, 1], first[:, 0])


def norm_body(far_count, step, *refs):
    total, first, gain = refs[:3]
    far, outs, framed = refs[3 : 3 + far_count], refs[3 + far_count : -1], refs[-1]
    level = lax.axis_index("row")
    mlp_out = total[...]
    for piece in far:
        mlp_out = mlp_out + piece[...].astype(jnp.float32)
    second = first[...].astype(jnp.float32) + norm_rows(mlp_out, gain[19:20].reshape(1, 1, -1))
    rows = second.shape[0]
    blank = jnp.zeros(framed.shape[1:], framed.dtype)
    framed[0] = blank
    framed[rows + 1] = blank
    framed[1 : rows + 1] = second.astype(jnp.bfloat16)
    for mask, out in enumerate(outs):
        out[...] = framed[pl.ds((level ^ mask) * step, step + 2)]


def conv_rows(field, kernel):
    frames, rows = field.shape[0] - 2, field.shape[1] - 2
    columns, width = field.shape[2:]
    share = kernel.shape[3]
    tokens = frames * rows * columns
    total = None
    for shift_time in range(3):
        for shift_row in range(3):
            slab = field[shift_time : shift_time + frames, shift_row : shift_row + rows]
            term = lax.dot_general(
                slab.reshape(tokens, width),
                kernel[shift_time, shift_row].reshape(3 * share, width),
                (((1,), (1,)), ((), ())),
                preferred_element_type=jnp.float32,
            )
            total = term if total is None else total + term
    column = lax.rem(lax.broadcasted_iota(jnp.int32, (tokens, share), 0), columns)
    before = jnp.where(column > 0, pltpu.roll(total[:, :share], 1, 0), 0.0)
    after = jnp.where(column < columns - 1, pltpu.roll(total[:, 2 * share :], tokens - 1, 0), 0.0)
    return (before + total[:, share : 2 * share] + after).reshape(frames, rows, columns, share)


def clear_ends(field):
    edge = jnp.zeros(field.shape[1:], field.dtype)
    field[0] = edge
    field[field.shape[0] - 1] = edge


def first_conv_body(height, *refs):
    kernel, hidden_ref, part_ref, field = refs[-4:]
    pieces = refs[:-4]
    count = len(pieces) // 2
    level, place = lax.axis_index("row"), lax.axis_index("frame")
    clear_ends(field)
    for index, piece in enumerate(pieces):
        frame = (level ^ (index % count)) + 1
        parity = half_of(place) ^ (index // count)
        for row in range(piece.shape[0]):
            field[frame, 2 * row + parity] = piece[row]
    activated = silu(conv_rows(field, kernel))
    frames, band, columns, share = hidden_ref.shape
    rows = band - 2
    global_row = level * rows - 1 + lax.broadcasted_iota(jnp.int32, activated.shape, 1)
    inside = (global_row >= 0) & (global_row < height)
    hidden_ref[...] = jnp.where(inside, activated, 0.0).astype(jnp.bfloat16)
    at = pl.multiple_of(place * share, share)
    part_ref[...] = field[1 : frames + 1, 2 : 2 + rows, :, pl.ds(at, share)]


def second_conv_body(*refs):
    pieces = refs[: (len(refs) - 4) // 2]
    part, kernel = refs[len(pieces) : len(pieces) + 2]
    outs, field, final = refs[len(pieces) + 2 : -2], refs[-2], refs[-1]
    place = lax.axis_index("frame")
    clear_ends(field)
    share = part.shape[3]
    frames = part.shape[0]
    for mask, piece in enumerate(pieces):
        at = pl.multiple_of((place ^ mask) * share, share)
        field[1 : frames + 1, :, :, pl.ds(at, share)] = piece[...]
    final[...] = part[...].astype(jnp.float32) + conv_rows(field, kernel)
    lines = final.shape[0] * final.shape[1]
    strip = outs[0].shape[0] // lines
    for mask, out in enumerate(outs):
        at = pl.multiple_of((place ^ mask) * strip, strip)
        out[...] = jnp.concatenate(
            [
                final[line // final.shape[1], line % final.shape[1], pl.ds(at, strip)]
                for line in range(lines)
            ],
            axis=0,
        ).astype(jnp.bfloat16)


def join_body(*refs):
    pieces, out_ref = refs[:-1], refs[-1]
    place = lax.axis_index("frame")
    share = pieces[0].shape[1]
    frames, rows, strip = out_ref.shape[:3]
    for mask, piece in enumerate(pieces):
        at = pl.multiple_of((place ^ mask) * share, share)
        cells = piece[...].astype(jnp.float32)
        for line in range(frames * rows):
            out_ref[line // rows, line % rows, :, pl.ds(at, share)] = cells[
                line * strip : (line + 1) * strip
            ].astype(jnp.bfloat16)


def by_frames(
    latent,
    qkv_weight,
    out_weight,
    attn_gain,
    in_weight,
    depth_weight,
    down_weight,
    mlp_gain,
    conv_first,
    conv_second,
):
    count = lax.axis_size("frame")
    place = lax.axis_index("frame")
    rows, columns, width = latent.shape[1:]
    height = rows * count
    tokens = height * columns
    share = qkv_weight.shape[1]
    units = down_weight.shape[0]
    half = height // 2
    bf16, f32 = jnp.bfloat16, jnp.float32
    own = latent.reshape(rows * columns, width)
    pieces = [None] * count
    masks = [1] + list(range(2, count, 2))
    for mask in masks:
        pairs = [
            (z * count + f, f * count + (z ^ mask)) for z in range(count) for f in range(count)
        ]
        pieces[mask] = lax.ppermute(own, ("row", "frame"), pairs)
    for mask in masks:
        pieces[mask ^ 1] = swap(pieces[mask], 1)
    out_pieces = gathered_by_mask(out_weight)
    weights = jnp.concatenate(
        [
            qkv_weight.reshape(3 * share, width),
            out_weight,
            down_weight,
            jnp.transpose(in_weight, (1, 0, 2)).reshape(-1, units),
        ]
    )
    taps = lax.dynamic_slice_in_dim(depth_weight, place * units, units, 3)
    scales = jnp.concatenate([taps.reshape(-1, units), attn_gain[None], mlp_gain[None]])
    mixed, cells = call(
        functools.partial(attend_body, count),
        [*pieces, weights],
        [((tokens, share), bf16), ((tokens, width), bf16)],
        flops=2 * tokens * width * 3 * share,
    )
    kept, sent, first = call(
        functools.partial(mlp_body, count, columns),
        [
            *gathered_by_mask(mixed),
            *out_pieces[1:],
            cells,
            weights,
            scales,
        ],
        [((half, columns, width), f32)] * 2 + [((half, columns, width), bf16)],
        scratch=[((tokens + 2 * columns, units), f32)],
        flops=2 * tokens * width * (width + 3 * units),
        room=8,
    )
    total = kept + swap(sent, 1)
    far = [swap(total.astype(bf16), mask) for mask in range(3, count, 2)]
    step = rows // 2
    windows = call(
        functools.partial(norm_body, len(far), step),
        [total, first, scales, *far],
        [((step + 2, columns, width), bf16)] * count,
        scratch=[((half + 2, columns, width), bf16)],
        flops=8 * total.size,
    )
    windows = list(windows)
    for mask in range(1, count):
        windows[mask] = lax.ppermute(windows[mask], "row", [(i, i ^ mask) for i in range(count)])
    others = [swap(window, 1) for window in windows]
    hidden, own_part = call(
        functools.partial(first_conv_body, height),
        [*windows, *others, conv_first],
        [((count, rows + 2, columns, share), bf16), ((count, rows, columns, share), bf16)],
        scratch=[((count + 2, rows + 4, columns, width), bf16)],
        flops=2 * count * (rows + 2) * columns * 27 * width * share,
        room=8,
    )
    strip = columns // count
    strips = call(
        second_conv_body,
        [*gathered_by_mask(hidden), own_part, conv_second],
        [((count * rows * strip, share), bf16)] * count,
        scratch=[
            ((count + 2, rows + 2, columns, width), bf16),
            ((count, rows, columns, share), f32),
        ],
        flops=2 * count * rows * columns * 27 * width * share,
        room=8,
    )
    outs = [strips[0]] + [swap(strips[mask], mask) for mask in range(1, count)]
    (decoded,) = call(join_body, outs, [((count, rows, strip, width), bf16)])
    return decoded


def solution(mesh):
    body = by_frames if mesh.shape["row"] == mesh.shape["frame"] else local
    in_specs = (
        P(("parts", "frame"), "row", None, None),
        P(None, "frame", None),
        P("frame", None),
        P(),
        P(None, None, "frame"),
        P(),
        P("frame", None),
        P(),
        P(None, None, None, "frame", None),
        P(None, None, None, "frame", None),
    )
    out_specs = P("parts", "row", "frame", None)
    return jax.shard_map(body, mesh=mesh, in_specs=in_specs, out_specs=out_specs, check_vma=False)
```

```python
import functools

import jax
import jax.numpy as jnp
from jax import lax
from jax.experimental import pallas as pl
from jax.experimental.pallas import tpu as pltpu
from jax.sharding import PartitionSpec as P

HEAD = 32


def padded_2(cells, sides, width):
    for axis, dim in sides:
        count = lax.axis_size(axis)
        ends = count - 1
        head = lax.slice_in_dim(cells, 0, width, axis=dim)
        tail = lax.slice_in_dim(cells, cells.shape[dim] - width, cells.shape[dim], axis=dim)
        cells = jnp.concatenate(
            [
                lax.ppermute(tail, axis, [(i, (i + 1) % count) for i in range(ends)]),
                cells,
                lax.ppermute(head, axis, [((i + 1) % count, i) for i in range(ends)]),
            ],
            axis=dim,
        )
    return cells


def norm_rows(values, gain):
    return values * lax.rsqrt(jnp.mean(values * values, axis=-1, keepdims=True) + 1e-05) * gain


def attend(packed):
    frames, height, columns = (packed.shape[0], packed.shape[1], packed.shape[2])
    width = packed.shape[4]
    heads = width // HEAD
    flat = packed.reshape(frames, height * columns, 3, heads, HEAD)
    query = jnp.maximum(flat[:, :, 0], 0)
    keys = jnp.maximum(flat[:, :, 1], 0)
    values = flat[:, :, 2]
    state = jnp.einsum("fnhd,fnhe->fhde", keys, values, preferred_element_type=jnp.float32)
    key_total = jnp.sum(keys.astype(jnp.float32), axis=1)
    state, key_total = (
        lax.psum(state.astype(jnp.bfloat16), "row").astype(jnp.float32),
        lax.psum(key_total.astype(jnp.bfloat16), "row").astype(jnp.float32),
    )
    count = height * lax.axis_size("row") * columns
    state = state / count
    key_mean = key_total / count
    query_wide = query.astype(jnp.float32)
    numer = jnp.einsum("fnhd,fhde->fnhe", query_wide, state, precision=lax.Precision.HIGHEST)
    denom = jnp.maximum(
        jnp.einsum("fnhd,fhd->fnh", query_wide, key_mean, precision=lax.Precision.HIGHEST), 1.0
    )
    return (numer / denom[..., None]).astype(jnp.bfloat16).reshape(frames, height, columns, width)


def depth_mix(inner, depth_local):
    height, columns = (inner.shape[1], inner.shape[2])
    extended = padded_2(inner, (("row", 1),), 1)
    padded = jnp.pad(extended, ((0, 0), (0, 0), (1, 1), (0, 0), (0, 0)))
    spread = jnp.zeros(inner.shape, jnp.float32)
    for shift_row in range(3):
        for shift_col in range(3):
            spread = (
                spread
                + padded[:, shift_row : shift_row + height, shift_col : shift_col + columns].astype(
                    jnp.float32
                )
                * depth_local[shift_row, shift_col]
            )
    return (spread[..., 0, :] * jax.nn.silu(spread[..., 1, :])).astype(jnp.bfloat16)


def conv_tile(extended, kernel):
    frames, padded_rows, columns, width = extended.shape
    height = padded_rows - 2
    out_width = kernel.shape[3]
    padded = jnp.pad(extended, ((1, 1), (0, 0), (1, 1), (0, 0)))
    result = jnp.zeros((frames * height * columns, out_width), jnp.float32)
    for shift_time in range(3):
        for shift_row in range(3):
            slab = padded[shift_time : shift_time + frames, shift_row : shift_row + height]
            stacked = jnp.stack(
                [slab[:, :, shift_col : shift_col + columns] for shift_col in range(3)], axis=3
            )
            result = result + jnp.einsum(
                "nci,coi->no",
                stacked.reshape(-1, 3, width),
                kernel[shift_time, shift_row],
                preferred_element_type=jnp.float32,
            )
    return result.reshape(frames, height, columns, out_width)


def local(
    latent,
    qkv_weight,
    out_weight,
    attn_gain,
    in_weight,
    depth_weight,
    down_weight,
    mlp_gain,
    conv_first,
    conv_second,
):
    frames, height, columns, width = latent.shape
    place = lax.axis_index("frame")
    packed = jnp.einsum(
        "frwc,kjc->frwkj",
        latent,
        lax.all_gather(qkv_weight, "frame", axis=1, tiled=True),
        preferred_element_type=jnp.float32,
    ).astype(jnp.bfloat16)
    mixed = attend(packed)
    section = mixed
    attn_out = jnp.einsum(
        "frwj,jc->frwc",
        section,
        lax.all_gather(out_weight, "frame", axis=0, tiled=True),
        preferred_element_type=jnp.float32,
    )
    first = (latent.astype(jnp.float32) + norm_rows(attn_out, attn_gain)).astype(jnp.bfloat16)
    inner = jax.nn.silu(
        jnp.einsum(
            "frwc,ckj->frwkj",
            first,
            lax.all_gather(in_weight, "frame", axis=2, tiled=True),
            preferred_element_type=jnp.float32,
        )
    ).astype(jnp.bfloat16)
    gated = depth_mix(inner, depth_weight)
    section = gated
    mlp_out = jnp.einsum(
        "frwj,jc->frwc",
        section,
        lax.all_gather(down_weight, "frame", axis=0, tiled=True),
        preferred_element_type=jnp.float32,
    )
    second = (first.astype(jnp.float32) + norm_rows(mlp_out, mlp_gain)).astype(jnp.bfloat16)
    gathered = lax.all_gather(second, "frame", axis=0, tiled=True)
    out_share = conv_first.shape[3]
    extended = padded_2(gathered, (("row", 1),), 2)
    activated = jax.nn.silu(conv_tile(extended, conv_first))
    global_row = lax.axis_index("row") * height - 1 + lax.iota(jnp.int32, height + 2)
    inside = ((global_row >= 0) & (global_row < height * lax.axis_size("row"))).astype(jnp.float32)
    hidden_conv = (activated * inside[None, :, None, None]).astype(jnp.bfloat16)
    joined = lax.all_gather(hidden_conv, "frame", axis=3, tiled=True)
    result = conv_tile(joined, conv_second)
    own_part = lax.dynamic_slice_in_dim(gathered, place * out_share, out_share, 3)
    final = (own_part.astype(jnp.float32) + result).astype(jnp.bfloat16)
    return lax.all_to_all(final, "frame", split_axis=2, concat_axis=3, tiled=True)


def swap(cells, mask):
    count = lax.axis_size("frame")
    return lax.ppermute(cells, "frame", [(i, i ^ mask) for i in range(count)])


def in_order(pieces, place, dim):
    step = 1
    while step < len(pieces):
        flip = (place & step) != 0
        pieces = [jnp.where(flip, pieces[i ^ step], pieces[i]) for i in range(len(pieces))]
        step *= 2
    return jnp.concatenate(pieces, axis=dim)


def gathered_by_mask(cells):
    count = lax.axis_size("frame")
    pieces = [None] * count
    pieces[0] = cells
    masks = list(range(3, count, 2))
    for mask in masks:
        pieces[mask] = swap(cells, mask)
    for mask in [0] + masks:
        pieces[mask ^ 1] = swap(pieces[mask], 1)
    return pieces


def silu(values):
    return values / (1.0 + jnp.exp(-values))


def half_of(place):
    return (place ^ (place >> 1)) & 1


def call(body, operands, outs, scratch=(), flops=0, room=4):
    moved = sum(o.size * o.dtype.itemsize for o in operands)
    return pl.pallas_call(
        body,
        out_shape=[jax.ShapeDtypeStruct(shape, kind) for shape, kind in outs],
        scratch_shapes=[pltpu.VMEM(shape, kind) for shape, kind in scratch],
        compiler_params=pltpu.CompilerParams(vmem_limit_bytes=room * 1024 * 1024),
        cost_estimate=pl.CostEstimate(flops=flops, bytes_accessed=moved, transcendentals=0),
    )(*operands)


def attend_body(count, *refs):
    pieces, (weight, mixed_ref, cells_ref) = refs[:count], refs[count:]
    place = lax.axis_index("frame")
    rows = pieces[0].shape[0]
    for mask, piece in enumerate(pieces):
        at = pl.multiple_of((place ^ mask) * rows, rows)
        cells_ref[pl.ds(at, rows)] = piece[...]
    tokens, share = mixed_ref.shape
    packed = lax.dot_general(
        cells_ref[...],
        weight[pl.ds(0, 3 * share)],
        (((1,), (1,)), ((), ())),
        preferred_element_type=jnp.float32,
    ).astype(jnp.bfloat16)
    query = jnp.maximum(packed[:, :share], 0)
    keys = jnp.maximum(packed[:, share : 2 * share], 0)
    values = packed[:, 2 * share :]
    joined = jnp.concatenate([values, jnp.ones_like(values)], axis=1)
    table = lax.dot_general(
        keys, joined, (((0,), (0,)), ((), ())), preferred_element_type=jnp.float32
    ) * (1.0 / tokens)
    head_in = lax.broadcasted_iota(jnp.int32, table.shape, 0) // HEAD
    head_out = lax.rem(lax.broadcasted_iota(jnp.int32, table.shape, 1), share) // HEAD
    table = jnp.where(head_in == head_out, table, 0.0)
    high = table.astype(jnp.bfloat16)
    low = (table - high.astype(jnp.float32)).astype(jnp.bfloat16)
    both = jnp.dot(query, high, preferred_element_type=jnp.float32) + jnp.dot(
        query, low, preferred_element_type=jnp.float32
    )
    mixed_ref[...] = (both[:, :share] / jnp.maximum(both[:, share:], 1.0)).astype(jnp.bfloat16)


def mlp_body(count, columns, *refs):
    mixed, out_weight = refs[:count], refs[count : 2 * count - 1]
    cells, weights, in_parts, scales, kept_ref, sent_ref, first_ref, field = refs[2 * count - 1 :]
    place = lax.axis_index("frame")
    tokens, width = cells.shape
    units = field.shape[1]
    share = mixed[0].shape[1]
    own_out, down = weights[pl.ds(3 * share, share)], weights[pl.ds(4 * share, units)]
    height = tokens // columns
    attn_out = sum(
        jnp.dot(a[...], b, preferred_element_type=jnp.float32)
        for a, b in zip(mixed, [own_out] + [piece[...] for piece in out_weight])
    )
    first = (cells[...].astype(jnp.float32) + norm_rows(attn_out, scales[18:19])).astype(jnp.bfloat16)
    column = lax.rem(lax.broadcasted_iota(jnp.int32, (tokens, units), 0), columns)
    blank = jnp.zeros((columns, units), jnp.float32)
    spread = []
    for part in range(2):
        inner = silu(jnp.dot(first, in_parts[part], preferred_element_type=jnp.float32))
        field[pl.ds(0, columns)] = blank
        field[pl.ds(columns, tokens)] = inner.astype(jnp.bfloat16).astype(jnp.float32)
        field[pl.ds(columns + tokens, columns)] = blank
        sides = []
        for shift_col in range(3):
            sides.append(
                sum(
                    field[pl.ds(shift_row * columns, tokens)]
                    * scales[tap : tap + 1]
                    for shift_row, tap in enumerate(range(2 * shift_col + part, 18, 6))
                )
            )
        spread.append(
            jnp.where(column > 0, pltpu.roll(sides[0], 1, 0), 0.0)
            + sides[1]
            + jnp.where(column < columns - 1, pltpu.roll(sides[2], tokens - 1, 0), 0.0)
        )
    gated = (spread[0] * silu(spread[1])).astype(jnp.bfloat16)
    partial = jnp.dot(gated, down, preferred_element_type=jnp.float32)
    partial = partial.reshape(height // 2, 2, columns, width)
    first = first.reshape(height // 2, 2, columns, width)
    odd = half_of(place) == 1
    kept_ref[...] = jnp.where(odd, partial[:, 1], partial[:, 0])
    sent_ref[...] = jnp.where(odd, partial[:, 0], partial[:, 1])
    first_ref[...] = jnp.where(odd, first[:, 1], first[:, 0])


def norm_body(far_count, step, *refs):
    total, first, gain = refs[:3]
    far, outs, framed = refs[3 : 3 + far_count], refs[3 + far_count : -1], refs[-1]
    level = lax.axis_index("row")
    mlp_out = total[...]
    for piece in far:
        mlp_out = mlp_out + piece[...].astype(jnp.float32)
    second = first[...].astype(jnp.float32) + norm_rows(mlp_out, gain[19:20].reshape(1, 1, -1))
    rows = second.shape[0]
    blank = jnp.zeros(framed.shape[1:], framed.dtype)
    framed[0] = blank
    framed[rows + 1] = blank
    framed[1 : rows + 1] = second.astype(jnp.bfloat16)
    for mask, out in enumerate(outs):
        out[...] = framed[pl.ds((level ^ mask) * step, step + 2)]


def conv_rows(field, kernel):
    frames, rows = field.shape[0] - 2, field.shape[1] - 2
    columns, width = field.shape[2:]
    share = kernel.shape[3]
    tokens = frames * rows * columns
    total = None
    for shift_time in range(3):
        for shift_row in range(3):
            slab = field[shift_time : shift_time + frames, shift_row : shift_row + rows]
            term = lax.dot_general(
                slab.reshape(tokens, width),
                kernel[shift_time, shift_row].reshape(3 * share, width),
                (((1,), (1,)), ((), ())),
                preferred_element_type=jnp.float32,
            )
            total = term if total is None else total + term
    column = lax.rem(lax.broadcasted_iota(jnp.int32, (tokens, share), 0), columns)
    before = jnp.where(column > 0, pltpu.roll(total[:, :share], 1, 0), 0.0)
    after = jnp.where(column < columns - 1, pltpu.roll(total[:, 2 * share :], tokens - 1, 0), 0.0)
    return (before + total[:, share : 2 * share] + after).reshape(frames, rows, columns, share)


def clear_ends(field):
    edge = jnp.zeros(field.shape[1:], field.dtype)
    field[0] = edge
    field[field.shape[0] - 1] = edge


def first_conv_body(height, *refs):
    kernel, hidden_ref, part_ref, field = refs[-4:]
    pieces = refs[:-4]
    count = len(pieces) // 2
    level, place = lax.axis_index("row"), lax.axis_index("frame")
    clear_ends(field)
    for index, piece in enumerate(pieces):
        frame = (level ^ (index % count)) + 1
        parity = half_of(place) ^ (index // count)
        for row in range(piece.shape[0]):
            field[frame, 2 * row + parity] = piece[row]
    activated = silu(conv_rows(field, kernel))
    frames, band, columns, share = hidden_ref.shape
    rows = band - 2
    global_row = level * rows - 1 + lax.broadcasted_iota(jnp.int32, activated.shape, 1)
    inside = (global_row >= 0) & (global_row < height)
    hidden_ref[...] = jnp.where(inside, activated, 0.0).astype(jnp.bfloat16)
    at = pl.multiple_of(place * share, share)
    part_ref[...] = field[1 : frames + 1, 2 : 2 + rows, :, pl.ds(at, share)]


def second_conv_body(*refs):
    pieces = refs[: (len(refs) - 4) // 2]
    part, kernel = refs[len(pieces) : len(pieces) + 2]
    outs, field, final = refs[len(pieces) + 2 : -2], refs[-2], refs[-1]
    place = lax.axis_index("frame")
    clear_ends(field)
    share = part.shape[3]
    frames = part.shape[0]
    for mask, piece in enumerate(pieces):
        at = pl.multiple_of((place ^ mask) * share, share)
        field[1 : frames + 1, :, :, pl.ds(at, share)] = piece[...]
    final[...] = part[...].astype(jnp.float32) + conv_rows(field, kernel)
    lines = final.shape[0] * final.shape[1]
    strip = outs[0].shape[0] // lines
    for mask, out in enumerate(outs):
        at = pl.multiple_of((place ^ mask) * strip, strip)
        out[...] = jnp.concatenate(
            [
                final[line // final.shape[1], line % final.shape[1], pl.ds(at, strip)]
                for line in range(lines)
            ],
            axis=0,
        ).astype(jnp.bfloat16)


def join_body(*refs):
    pieces, out_ref = refs[:-1], refs[-1]
    place = lax.axis_index("frame")
    share = pieces[0].shape[1]
    frames, rows, strip = out_ref.shape[:3]
    for mask, piece in enumerate(pieces):
        at = pl.multiple_of((place ^ mask) * share, share)
        cells = piece[...].astype(jnp.float32)
        for line in range(frames * rows):
            out_ref[line // rows, line % rows, :, pl.ds(at, share)] = cells[
                line * strip : (line + 1) * strip
            ].astype(jnp.bfloat16)


def by_frames(
    latent,
    qkv_weight,
    out_weight,
    attn_gain,
    in_weight,
    depth_weight,
    down_weight,
    mlp_gain,
    conv_first,
    conv_second,
):
    count = lax.axis_size("frame")
    place = lax.axis_index("frame")
    rows, columns, width = latent.shape[1:]
    height = rows * count
    tokens = height * columns
    share = qkv_weight.shape[1]
    units = down_weight.shape[0]
    half = height // 2
    bf16, f32 = jnp.bfloat16, jnp.float32
    own = latent.reshape(rows * columns, width)
    pieces = [None] * count
    masks = [1] + list(range(2, count, 2))
    for mask in masks:
        pairs = [
            (z * count + f, f * count + (z ^ mask)) for z in range(count) for f in range(count)
        ]
        pieces[mask] = lax.ppermute(own, ("row", "frame"), pairs)
    for mask in masks:
        pieces[mask ^ 1] = swap(pieces[mask], 1)
    out_pieces = gathered_by_mask(out_weight)
    weights = jnp.concatenate([qkv_weight.reshape(3 * share, width), out_weight, down_weight])
    in_parts = jnp.transpose(in_weight, (1, 0, 2))
    taps = lax.dynamic_slice_in_dim(depth_weight, place * units, units, 3)
    scales = jnp.concatenate([taps.reshape(-1, units), attn_gain[None], mlp_gain[None]])
    mixed, cells = call(
        functools.partial(attend_body, count),
        [*pieces, weights],
        [((tokens, share), bf16), ((tokens, width), bf16)],
        flops=2 * tokens * width * 3 * share,
    )
    kept, sent, first = call(
        functools.partial(mlp_body, count, columns),
        [
            *gathered_by_mask(mixed),
            *out_pieces[1:],
            cells,
            weights,
            in_parts,
            scales,
        ],
        [((half, columns, width), f32)] * 2 + [((half, columns, width), bf16)],
        scratch=[((tokens + 2 * columns, units), f32)],
        flops=2 * tokens * width * (width + 3 * units),
        room=8,
    )
    total = kept + swap(sent, 1)
    far = [swap(total.astype(bf16), mask) for mask in range(3, count, 2)]
    step = rows // 2
    windows = call(
        functools.partial(norm_body, len(far), step),
        [total, first, scales, *far],
        [((step + 2, columns, width), bf16)] * count,
        scratch=[((half + 2, columns, width), bf16)],
        flops=8 * total.size,
    )
    windows = list(windows)
    for mask in reversed(range(1, count)):
        windows[mask] = lax.ppermute(windows[mask], "row", [(i, i ^ mask) for i in range(count)])
    others = [swap(window, 1) for window in windows]
    hidden, own_part = call(
        functools.partial(first_conv_body, height),
        [*windows, *others, conv_first],
        [((count, rows + 2, columns, share), bf16), ((count, rows, columns, share), bf16)],
        scratch=[((count + 2, rows + 4, columns, width), bf16)],
        flops=2 * count * (rows + 2) * columns * 27 * width * share,
        room=8,
    )
    strip = columns // count
    strips = call(
        second_conv_body,
        [*gathered_by_mask(hidden), own_part, conv_second],
        [((count * rows * strip, share), bf16)] * count,
        scratch=[
            ((count + 2, rows + 2, columns, width), bf16),
            ((count, rows, columns, share), f32),
        ],
        flops=2 * count * rows * columns * 27 * width * share,
        room=8,
    )
    outs = [strips[0]] + [swap(strips[mask], mask) for mask in range(1, count)]
    (decoded,) = call(join_body, outs, [((count, rows, strip, width), bf16)])
    return decoded


def solution(mesh):
    body = by_frames if mesh.shape["row"] == mesh.shape["frame"] else local
    in_specs = (
        P(("parts", "frame"), "row", None, None),
        P(None, "frame", None),
        P("frame", None),
        P(),
        P(None, None, "frame"),
        P(),
        P("frame", None),
        P(),
        P(None, None, None, "frame", None),
        P(None, None, None, "frame", None),
    )
    out_specs = P("parts", "row", "frame", None)
    return jax.shard_map(body, mesh=mesh, in_specs=in_specs, out_specs=out_specs, check_vma=False)
```

```python
import functools

import jax
import jax.numpy as jnp
from jax import lax
from jax.experimental import pallas as pl
from jax.experimental.pallas import tpu as pltpu
from jax.sharding import PartitionSpec as P

HEAD = 32


def padded_2(cells, sides, width):
    for axis, dim in sides:
        count = lax.axis_size(axis)
        ends = count - 1
        head = lax.slice_in_dim(cells, 0, width, axis=dim)
        tail = lax.slice_in_dim(cells, cells.shape[dim] - width, cells.shape[dim], axis=dim)
        cells = jnp.concatenate(
            [
                lax.ppermute(tail, axis, [(i, (i + 1) % count) for i in range(ends)]),
                cells,
                lax.ppermute(head, axis, [((i + 1) % count, i) for i in range(ends)]),
            ],
            axis=dim,
        )
    return cells


def norm_rows(values, gain):
    return values * lax.rsqrt(jnp.mean(values * values, axis=-1, keepdims=True) + 1e-05) * gain


def attend(packed):
    frames, height, columns = (packed.shape[0], packed.shape[1], packed.shape[2])
    width = packed.shape[4]
    heads = width // HEAD
    flat = packed.reshape(frames, height * columns, 3, heads, HEAD)
    query = jnp.maximum(flat[:, :, 0], 0)
    keys = jnp.maximum(flat[:, :, 1], 0)
    values = flat[:, :, 2]
    state = jnp.einsum("fnhd,fnhe->fhde", keys, values, preferred_element_type=jnp.float32)
    key_total = jnp.sum(keys.astype(jnp.float32), axis=1)
    state, key_total = (
        lax.psum(state.astype(jnp.bfloat16), "row").astype(jnp.float32),
        lax.psum(key_total.astype(jnp.bfloat16), "row").astype(jnp.float32),
    )
    count = height * lax.axis_size("row") * columns
    state = state / count
    key_mean = key_total / count
    query_wide = query.astype(jnp.float32)
    numer = jnp.einsum("fnhd,fhde->fnhe", query_wide, state, precision=lax.Precision.HIGHEST)
    denom = jnp.maximum(
        jnp.einsum("fnhd,fhd->fnh", query_wide, key_mean, precision=lax.Precision.HIGHEST), 1.0
    )
    return (numer / denom[..., None]).astype(jnp.bfloat16).reshape(frames, height, columns, width)


def depth_mix(inner, depth_local):
    height, columns = (inner.shape[1], inner.shape[2])
    extended = padded_2(inner, (("row", 1),), 1)
    padded = jnp.pad(extended, ((0, 0), (0, 0), (1, 1), (0, 0), (0, 0)))
    spread = jnp.zeros(inner.shape, jnp.float32)
    for shift_row in range(3):
        for shift_col in range(3):
            spread = (
                spread
                + padded[:, shift_row : shift_row + height, shift_col : shift_col + columns].astype(
                    jnp.float32
                )
                * depth_local[shift_row, shift_col]
            )
    return (spread[..., 0, :] * jax.nn.silu(spread[..., 1, :])).astype(jnp.bfloat16)


def conv_tile(extended, kernel):
    frames, padded_rows, columns, width = extended.shape
    height = padded_rows - 2
    out_width = kernel.shape[3]
    padded = jnp.pad(extended, ((1, 1), (0, 0), (1, 1), (0, 0)))
    result = jnp.zeros((frames * height * columns, out_width), jnp.float32)
    for shift_time in range(3):
        for shift_row in range(3):
            slab = padded[shift_time : shift_time + frames, shift_row : shift_row + height]
            stacked = jnp.stack(
                [slab[:, :, shift_col : shift_col + columns] for shift_col in range(3)], axis=3
            )
            result = result + jnp.einsum(
                "nci,coi->no",
                stacked.reshape(-1, 3, width),
                kernel[shift_time, shift_row],
                preferred_element_type=jnp.float32,
            )
    return result.reshape(frames, height, columns, out_width)


def local(
    latent,
    qkv_weight,
    out_weight,
    attn_gain,
    in_weight,
    depth_weight,
    down_weight,
    mlp_gain,
    conv_first,
    conv_second,
):
    frames, height, columns, width = latent.shape
    place = lax.axis_index("frame")
    packed = jnp.einsum(
        "frwc,kjc->frwkj",
        latent,
        lax.all_gather(qkv_weight, "frame", axis=1, tiled=True),
        preferred_element_type=jnp.float32,
    ).astype(jnp.bfloat16)
    mixed = attend(packed)
    section = mixed
    attn_out = jnp.einsum(
        "frwj,jc->frwc",
        section,
        lax.all_gather(out_weight, "frame", axis=0, tiled=True),
        preferred_element_type=jnp.float32,
    )
    first = (latent.astype(jnp.float32) + norm_rows(attn_out, attn_gain)).astype(jnp.bfloat16)
    inner = jax.nn.silu(
        jnp.einsum(
            "frwc,ckj->frwkj",
            first,
            lax.all_gather(in_weight, "frame", axis=2, tiled=True),
            preferred_element_type=jnp.float32,
        )
    ).astype(jnp.bfloat16)
    gated = depth_mix(inner, depth_weight)
    section = gated
    mlp_out = jnp.einsum(
        "frwj,jc->frwc",
        section,
        lax.all_gather(down_weight, "frame", axis=0, tiled=True),
        preferred_element_type=jnp.float32,
    )
    second = (first.astype(jnp.float32) + norm_rows(mlp_out, mlp_gain)).astype(jnp.bfloat16)
    gathered = lax.all_gather(second, "frame", axis=0, tiled=True)
    out_share = conv_first.shape[3]
    extended = padded_2(gathered, (("row", 1),), 2)
    activated = jax.nn.silu(conv_tile(extended, conv_first))
    global_row = lax.axis_index("row") * height - 1 + lax.iota(jnp.int32, height + 2)
    inside = ((global_row >= 0) & (global_row < height * lax.axis_size("row"))).astype(jnp.float32)
    hidden_conv = (activated * inside[None, :, None, None]).astype(jnp.bfloat16)
    joined = lax.all_gather(hidden_conv, "frame", axis=3, tiled=True)
    result = conv_tile(joined, conv_second)
    own_part = lax.dynamic_slice_in_dim(gathered, place * out_share, out_share, 3)
    final = (own_part.astype(jnp.float32) + result).astype(jnp.bfloat16)
    return lax.all_to_all(final, "frame", split_axis=2, concat_axis=3, tiled=True)


def swap(cells, mask):
    count = lax.axis_size("frame")
    return lax.ppermute(cells, "frame", [(i, i ^ mask) for i in range(count)])


def in_order(pieces, place, dim):
    step = 1
    while step < len(pieces):
        flip = (place & step) != 0
        pieces = [jnp.where(flip, pieces[i ^ step], pieces[i]) for i in range(len(pieces))]
        step *= 2
    return jnp.concatenate(pieces, axis=dim)


def gathered_by_mask(cells):
    count = lax.axis_size("frame")
    pieces = [None] * count
    pieces[0] = cells
    masks = list(range(3, count, 2))
    for mask in masks:
        pieces[mask] = swap(cells, mask)
    for mask in [0] + masks:
        pieces[mask ^ 1] = swap(pieces[mask], 1)
    return pieces


def silu(values):
    return values / (1.0 + jnp.exp(-values))


def half_of(place):
    return (place ^ (place >> 1)) & 1


def call(body, operands, outs, scratch=(), flops=0, room=4):
    moved = sum(o.size * o.dtype.itemsize for o in operands)
    return pl.pallas_call(
        body,
        out_shape=[jax.ShapeDtypeStruct(shape, kind) for shape, kind in outs],
        scratch_shapes=[pltpu.VMEM(shape, kind) for shape, kind in scratch],
        compiler_params=pltpu.CompilerParams(vmem_limit_bytes=room * 1024 * 1024),
        cost_estimate=pl.CostEstimate(flops=flops, bytes_accessed=moved, transcendentals=0),
    )(*operands)


def attend_body(count, *refs):
    pieces, (weight, mixed_ref, cells_ref) = refs[:count], refs[count:]
    place = lax.axis_index("frame")
    rows = pieces[0].shape[0]
    for mask, piece in enumerate(pieces):
        at = pl.multiple_of((place ^ mask) * rows, rows)
        cells_ref[pl.ds(at, rows)] = piece[...]
    tokens, share = mixed_ref.shape
    packed = lax.dot_general(
        cells_ref[...],
        weight[pl.ds(0, 3 * share)],
        (((1,), (1,)), ((), ())),
        preferred_element_type=jnp.float32,
    ).astype(jnp.bfloat16)
    query = jnp.maximum(packed[:, :share], 0)
    keys = jnp.maximum(packed[:, share : 2 * share], 0)
    values = packed[:, 2 * share :]
    joined = jnp.concatenate([values, jnp.ones_like(values)], axis=1)
    table = lax.dot_general(
        keys, joined, (((0,), (0,)), ((), ())), preferred_element_type=jnp.float32
    ) * (1.0 / tokens)
    head_in = lax.broadcasted_iota(jnp.int32, table.shape, 0) // HEAD
    head_out = lax.rem(lax.broadcasted_iota(jnp.int32, table.shape, 1), share) // HEAD
    table = jnp.where(head_in == head_out, table, 0.0)
    high = table.astype(jnp.bfloat16)
    low = (table - high.astype(jnp.float32)).astype(jnp.bfloat16)
    both = jnp.dot(query, high, preferred_element_type=jnp.float32) + jnp.dot(
        query, low, preferred_element_type=jnp.float32
    )
    mixed_ref[...] = (both[:, :share] / jnp.maximum(both[:, share:], 1.0)).astype(jnp.bfloat16)


def mlp_body(count, columns, *refs):
    mixed, out_weight = refs[:count], refs[count : 2 * count - 1]
    cells, weights, in_parts, scales, kept_ref, sent_ref, first_ref, field = refs[2 * count - 1 :]
    place = lax.axis_index("frame")
    tokens, width = cells.shape
    units = field.shape[1]
    share = mixed[0].shape[1]
    own_out, down = weights[pl.ds(3 * share, share)], weights[pl.ds(4 * share, units)]
    height = tokens // columns
    attn_out = sum(
        jnp.dot(a[...], b, preferred_element_type=jnp.float32)
        for a, b in zip(mixed, [own_out] + [piece[...] for piece in out_weight])
    )
    first = (cells[...].astype(jnp.float32) + norm_rows(attn_out, scales[18:19])).astype(jnp.bfloat16)
    column = lax.rem(lax.broadcasted_iota(jnp.int32, (tokens, units), 0), columns)
    blank = jnp.zeros((columns, units), jnp.float32)
    spread = []
    for part in range(2):
        inner = silu(jnp.dot(first, in_parts[part], preferred_element_type=jnp.float32))
        field[pl.ds(0, columns)] = blank
        field[pl.ds(columns, tokens)] = inner.astype(jnp.bfloat16).astype(jnp.float32)
        field[pl.ds(columns + tokens, columns)] = blank
        sides = []
        for shift_col in range(3):
            sides.append(
                sum(
                    field[pl.ds(shift_row * columns, tokens)]
                    * scales[tap : tap + 1]
                    for shift_row, tap in enumerate(range(2 * shift_col + part, 18, 6))
                )
            )
        spread.append(
            jnp.where(column > 0, pltpu.roll(sides[0], 1, 0), 0.0)
            + sides[1]
            + jnp.where(column < columns - 1, pltpu.roll(sides[2], tokens - 1, 0), 0.0)
        )
    gated = (spread[0] * silu(spread[1])).astype(jnp.bfloat16)
    partial = jnp.dot(gated, down, preferred_element_type=jnp.float32)
    partial = partial.reshape(height // 2, 2, columns, width)
    first = first.reshape(height // 2, 2, columns, width)
    odd = half_of(place) == 1
    kept_ref[...] = jnp.where(odd, partial[:, 1], partial[:, 0])
    sent_ref[...] = jnp.where(odd, partial[:, 0], partial[:, 1])
    first_ref[...] = jnp.where(odd, first[:, 1], first[:, 0])


def norm_body(far_count, step, *refs):
    total, first, gain = refs[:3]
    far, outs, framed = refs[3 : 3 + far_count], refs[3 + far_count : -1], refs[-1]
    level = lax.axis_index("row")
    mlp_out = total[...]
    for piece in far:
        mlp_out = mlp_out + piece[...].astype(jnp.float32)
    second = first[...].astype(jnp.float32) + norm_rows(mlp_out, gain[19:20].reshape(1, 1, -1))
    rows = second.shape[0]
    blank = jnp.zeros(framed.shape[1:], framed.dtype)
    framed[0] = blank
    framed[rows + 1] = blank
    framed[1 : rows + 1] = second.astype(jnp.bfloat16)
    for mask, out in enumerate(outs):
        out[...] = framed[pl.ds(lax.rem(level + mask, len(outs)) * step, step + 2)]


def conv_rows(field, kernel):
    frames, rows = field.shape[0] - 2, field.shape[1] - 2
    columns, width = field.shape[2:]
    share = kernel.shape[3]
    tokens = frames * rows * columns
    total = None
    for shift_time in range(3):
        for shift_row in range(3):
            slab = field[shift_time : shift_time + frames, shift_row : shift_row + rows]
            term = lax.dot_general(
                slab.reshape(tokens, width),
                kernel[shift_time, shift_row].reshape(3 * share, width),
                (((1,), (1,)), ((), ())),
                preferred_element_type=jnp.float32,
            )
            total = term if total is None else total + term
    column = lax.rem(lax.broadcasted_iota(jnp.int32, (tokens, share), 0), columns)
    before = jnp.where(column > 0, pltpu.roll(total[:, :share], 1, 0), 0.0)
    after = jnp.where(column < columns - 1, pltpu.roll(total[:, 2 * share :], tokens - 1, 0), 0.0)
    return (before + total[:, share : 2 * share] + after).reshape(frames, rows, columns, share)


def clear_ends(field):
    edge = jnp.zeros(field.shape[1:], field.dtype)
    field[0] = edge
    field[field.shape[0] - 1] = edge


def first_conv_body(height, *refs):
    kernel, hidden_ref, part_ref, field = refs[-4:]
    pieces = refs[:-4]
    count = len(pieces) // 2
    level, place = lax.axis_index("row"), lax.axis_index("frame")
    clear_ends(field)
    for index, piece in enumerate(pieces):
        frame = lax.rem(level + count - index % count, count) + 1
        parity = half_of(place) ^ (index // count)
        for row in range(piece.shape[0]):
            field[frame, 2 * row + parity] = piece[row]
    activated = silu(conv_rows(field, kernel))
    frames, band, columns, share = hidden_ref.shape
    rows = band - 2
    global_row = level * rows - 1 + lax.broadcasted_iota(jnp.int32, activated.shape, 1)
    inside = (global_row >= 0) & (global_row < height)
    hidden_ref[...] = jnp.where(inside, activated, 0.0).astype(jnp.bfloat16)
    at = pl.multiple_of(place * share, share)
    part_ref[...] = field[1 : frames + 1, 2 : 2 + rows, :, pl.ds(at, share)]


def second_conv_body(*refs):
    pieces = refs[: (len(refs) - 4) // 2]
    part, kernel = refs[len(pieces) : len(pieces) + 2]
    outs, field, final = refs[len(pieces) + 2 : -2], refs[-2], refs[-1]
    place = lax.axis_index("frame")
    clear_ends(field)
    share = part.shape[3]
    frames = part.shape[0]
    for mask, piece in enumerate(pieces):
        at = pl.multiple_of((place ^ mask) * share, share)
        field[1 : frames + 1, :, :, pl.ds(at, share)] = piece[...]
    final[...] = part[...].astype(jnp.float32) + conv_rows(field, kernel)
    lines = final.shape[0] * final.shape[1]
    strip = outs[0].shape[0] // lines
    for mask, out in enumerate(outs):
        at = pl.multiple_of(lax.rem(place + mask, len(outs)) * strip, strip)
        out[...] = jnp.concatenate(
            [
                final[line // final.shape[1], line % final.shape[1], pl.ds(at, strip)]
                for line in range(lines)
            ],
            axis=0,
        ).astype(jnp.bfloat16)


def join_body(*refs):
    pieces, out_ref = refs[:-1], refs[-1]
    place = lax.axis_index("frame")
    share = pieces[0].shape[1]
    frames, rows, strip = out_ref.shape[:3]
    for mask, piece in enumerate(pieces):
        at = pl.multiple_of(lax.rem(place + len(pieces) - mask, len(pieces)) * share, share)
        cells = piece[...].astype(jnp.float32)
        for line in range(frames * rows):
            out_ref[line // rows, line % rows, :, pl.ds(at, share)] = cells[
                line * strip : (line + 1) * strip
            ].astype(jnp.bfloat16)


def by_frames(
    latent,
    qkv_weight,
    out_weight,
    attn_gain,
    in_weight,
    depth_weight,
    down_weight,
    mlp_gain,
    conv_first,
    conv_second,
):
    count = lax.axis_size("frame")
    place = lax.axis_index("frame")
    rows, columns, width = latent.shape[1:]
    height = rows * count
    tokens = height * columns
    share = qkv_weight.shape[1]
    units = down_weight.shape[0]
    half = height // 2
    bf16, f32 = jnp.bfloat16, jnp.float32
    own = latent.reshape(rows * columns, width)
    pieces = [None] * count
    masks = [*range(3, count, 2), 1]
    for mask in masks:
        pairs = [
            (z * count + f, f * count + (z ^ mask)) for z in range(count) for f in range(count)
        ]
        pieces[mask] = lax.ppermute(own, ("row", "frame"), pairs)
    weights = jnp.concatenate([qkv_weight.reshape(3 * share, width), out_weight, down_weight])
    in_parts = jnp.transpose(in_weight, (1, 0, 2))
    *arrived, weights = lax.optimization_barrier((*[pieces[mask] for mask in masks], weights))
    for mask, piece in zip(masks, arrived):
        pieces[mask], pieces[mask ^ 1] = piece, swap(piece, 1)
    out_pieces = gathered_by_mask(out_weight)
    taps = lax.dynamic_slice_in_dim(depth_weight, place * units, units, 3)
    scales = jnp.concatenate([taps.reshape(-1, units), attn_gain[None], mlp_gain[None]])
    mixed, cells = call(
        functools.partial(attend_body, count),
        [*pieces, weights],
        [((tokens, share), bf16), ((tokens, width), bf16)],
        flops=2 * tokens * width * 3 * share,
    )
    kept, sent, first = call(
        functools.partial(mlp_body, count, columns),
        [
            *gathered_by_mask(mixed),
            *out_pieces[1:],
            cells,
            weights,
            in_parts,
            scales,
        ],
        [((half, columns, width), f32)] * 2 + [((half, columns, width), bf16)],
        scratch=[((tokens + 2 * columns, units), f32)],
        flops=2 * tokens * width * (width + 3 * units),
        room=8,
    )
    total = kept + swap(sent, 1)
    far = [swap(total.astype(bf16), mask) for mask in range(3, count, 2)]
    step = rows // 2
    windows = call(
        functools.partial(norm_body, len(far), step),
        [total, first, scales, *far],
        [((step + 2, columns, width), bf16)] * count,
        scratch=[((half + 2, columns, width), bf16)],
        flops=8 * total.size,
    )
    windows = list(windows)
    for mask in (1, 2, 3):
        pairs = [(i, (i + mask) % count) for i in range(count)]
        windows[mask] = lax.ppermute(windows[mask], "row", pairs)
    others = [swap(window, 1) for window in windows]
    hidden, own_part = call(
        functools.partial(first_conv_body, height),
        [*windows, *others, conv_first],
        [((count, rows + 2, columns, share), bf16), ((count, rows, columns, share), bf16)],
        scratch=[((count + 2, rows + 4, columns, width), bf16)],
        flops=2 * count * (rows + 2) * columns * 27 * width * share,
        room=8,
    )
    strip = columns // count
    strips = call(
        second_conv_body,
        [*gathered_by_mask(hidden), own_part, conv_second],
        [((count * rows * strip, share), bf16)] * count,
        scratch=[
            ((count + 2, rows + 2, columns, width), bf16),
            ((count, rows, columns, share), f32),
        ],
        flops=2 * count * rows * columns * 27 * width * share,
        room=8,
    )
    outs = list(strips)
    for mask in (2, 1, 3):
        pairs = [(i, (i + mask) % count) for i in range(count)]
        outs[mask] = lax.ppermute(strips[mask], "frame", pairs)
    (decoded,) = call(join_body, outs, [((count, rows, strip, width), bf16)])
    return decoded


def solution(mesh):
    body = by_frames if mesh.shape["row"] == mesh.shape["frame"] else local
    in_specs = (
        P(("parts", "frame"), "row", None, None),
        P(None, "frame", None),
        P("frame", None),
        P(),
        P(None, None, "frame"),
        P(),
        P("frame", None),
        P(),
        P(None, None, None, "frame", None),
        P(None, None, None, "frame", None),
    )
    out_specs = P("parts", "row", "frame", None)
    return jax.shard_map(body, mesh=mesh, in_specs=in_specs, out_specs=out_specs, check_vma=False)
```

```python
import functools

import jax
import jax.numpy as jnp
from jax import lax
from jax.experimental import pallas as pl
from jax.experimental.pallas import tpu as pltpu
from jax.sharding import PartitionSpec as P

HEAD = 32


def padded_2(cells, sides, width):
    for axis, dim in sides:
        count = lax.axis_size(axis)
        ends = count - 1
        head = lax.slice_in_dim(cells, 0, width, axis=dim)
        tail = lax.slice_in_dim(cells, cells.shape[dim] - width, cells.shape[dim], axis=dim)
        cells = jnp.concatenate(
            [
                lax.ppermute(tail, axis, [(i, (i + 1) % count) for i in range(ends)]),
                cells,
                lax.ppermute(head, axis, [((i + 1) % count, i) for i in range(ends)]),
            ],
            axis=dim,
        )
    return cells


def norm_rows(values, gain):
    return values * lax.rsqrt(jnp.mean(values * values, axis=-1, keepdims=True) + 1e-05) * gain


def attend(packed):
    frames, height, columns = (packed.shape[0], packed.shape[1], packed.shape[2])
    width = packed.shape[4]
    heads = width // HEAD
    flat = packed.reshape(frames, height * columns, 3, heads, HEAD)
    query = jnp.maximum(flat[:, :, 0], 0)
    keys = jnp.maximum(flat[:, :, 1], 0)
    values = flat[:, :, 2]
    state = jnp.einsum("fnhd,fnhe->fhde", keys, values, preferred_element_type=jnp.float32)
    key_total = jnp.sum(keys.astype(jnp.float32), axis=1)
    state, key_total = (
        lax.psum(state.astype(jnp.bfloat16), "row").astype(jnp.float32),
        lax.psum(key_total.astype(jnp.bfloat16), "row").astype(jnp.float32),
    )
    count = height * lax.axis_size("row") * columns
    state = state / count
    key_mean = key_total / count
    query_wide = query.astype(jnp.float32)
    numer = jnp.einsum("fnhd,fhde->fnhe", query_wide, state, precision=lax.Precision.HIGHEST)
    denom = jnp.maximum(
        jnp.einsum("fnhd,fhd->fnh", query_wide, key_mean, precision=lax.Precision.HIGHEST), 1.0
    )
    return (numer / denom[..., None]).astype(jnp.bfloat16).reshape(frames, height, columns, width)


def depth_mix(inner, depth_local):
    height, columns = (inner.shape[1], inner.shape[2])
    extended = padded_2(inner, (("row", 1),), 1)
    padded = jnp.pad(extended, ((0, 0), (0, 0), (1, 1), (0, 0), (0, 0)))
    spread = jnp.zeros(inner.shape, jnp.float32)
    for shift_row in range(3):
        for shift_col in range(3):
            spread = (
                spread
                + padded[:, shift_row : shift_row + height, shift_col : shift_col + columns].astype(
                    jnp.float32
                )
                * depth_local[shift_row, shift_col]
            )
    return (spread[..., 0, :] * jax.nn.silu(spread[..., 1, :])).astype(jnp.bfloat16)


def conv_tile(extended, kernel):
    frames, padded_rows, columns, width = extended.shape
    height = padded_rows - 2
    out_width = kernel.shape[3]
    padded = jnp.pad(extended, ((1, 1), (0, 0), (1, 1), (0, 0)))
    result = jnp.zeros((frames * height * columns, out_width), jnp.float32)
    for shift_time in range(3):
        for shift_row in range(3):
            slab = padded[shift_time : shift_time + frames, shift_row : shift_row + height]
            stacked = jnp.stack(
                [slab[:, :, shift_col : shift_col + columns] for shift_col in range(3)], axis=3
            )
            result = result + jnp.einsum(
                "nci,coi->no",
                stacked.reshape(-1, 3, width),
                kernel[shift_time, shift_row],
                preferred_element_type=jnp.float32,
            )
    return result.reshape(frames, height, columns, out_width)


def local(
    latent,
    qkv_weight,
    out_weight,
    attn_gain,
    in_weight,
    depth_weight,
    down_weight,
    mlp_gain,
    conv_first,
    conv_second,
):
    frames, height, columns, width = latent.shape
    place = lax.axis_index("frame")
    packed = jnp.einsum(
        "frwc,kjc->frwkj",
        latent,
        lax.all_gather(qkv_weight, "frame", axis=1, tiled=True),
        preferred_element_type=jnp.float32,
    ).astype(jnp.bfloat16)
    mixed = attend(packed)
    section = mixed
    attn_out = jnp.einsum(
        "frwj,jc->frwc",
        section,
        lax.all_gather(out_weight, "frame", axis=0, tiled=True),
        preferred_element_type=jnp.float32,
    )
    first = (latent.astype(jnp.float32) + norm_rows(attn_out, attn_gain)).astype(jnp.bfloat16)
    inner = jax.nn.silu(
        jnp.einsum(
            "frwc,ckj->frwkj",
            first,
            lax.all_gather(in_weight, "frame", axis=2, tiled=True),
            preferred_element_type=jnp.float32,
        )
    ).astype(jnp.bfloat16)
    gated = depth_mix(inner, depth_weight)
    section = gated
    mlp_out = jnp.einsum(
        "frwj,jc->frwc",
        section,
        lax.all_gather(down_weight, "frame", axis=0, tiled=True),
        preferred_element_type=jnp.float32,
    )
    second = (first.astype(jnp.float32) + norm_rows(mlp_out, mlp_gain)).astype(jnp.bfloat16)
    gathered = lax.all_gather(second, "frame", axis=0, tiled=True)
    out_share = conv_first.shape[3]
    extended = padded_2(gathered, (("row", 1),), 2)
    activated = jax.nn.silu(conv_tile(extended, conv_first))
    global_row = lax.axis_index("row") * height - 1 + lax.iota(jnp.int32, height + 2)
    inside = ((global_row >= 0) & (global_row < height * lax.axis_size("row"))).astype(jnp.float32)
    hidden_conv = (activated * inside[None, :, None, None]).astype(jnp.bfloat16)
    joined = lax.all_gather(hidden_conv, "frame", axis=3, tiled=True)
    result = conv_tile(joined, conv_second)
    own_part = lax.dynamic_slice_in_dim(gathered, place * out_share, out_share, 3)
    final = (own_part.astype(jnp.float32) + result).astype(jnp.bfloat16)
    return lax.all_to_all(final, "frame", split_axis=2, concat_axis=3, tiled=True)


def swap(cells, mask):
    count = lax.axis_size("frame")
    return lax.ppermute(cells, "frame", [(i, i ^ mask) for i in range(count)])


def in_order(pieces, place, dim):
    step = 1
    while step < len(pieces):
        flip = (place & step) != 0
        pieces = [jnp.where(flip, pieces[i ^ step], pieces[i]) for i in range(len(pieces))]
        step *= 2
    return jnp.concatenate(pieces, axis=dim)


def gathered_by_mask(cells):
    count = lax.axis_size("frame")
    pieces = [None] * count
    pieces[0] = cells
    masks = list(range(3, count, 2))
    for mask in masks:
        pieces[mask] = swap(cells, mask)
    for mask in [0] + masks:
        pieces[mask ^ 1] = swap(pieces[mask], 1)
    return pieces


def silu(values):
    return values / (1.0 + jnp.exp(-values))


def half_of(place):
    return (place ^ (place >> 1)) & 1


def call(body, operands, outs, scratch=(), flops=0, room=4):
    moved = sum(o.size * o.dtype.itemsize for o in operands)
    return pl.pallas_call(
        body,
        out_shape=[jax.ShapeDtypeStruct(shape, kind) for shape, kind in outs],
        scratch_shapes=[pltpu.VMEM(shape, kind) for shape, kind in scratch],
        compiler_params=pltpu.CompilerParams(vmem_limit_bytes=room * 1024 * 1024),
        cost_estimate=pl.CostEstimate(flops=flops, bytes_accessed=moved, transcendentals=0),
    )(*operands)


def attend_body(count, *refs):
    pieces, (weight, mixed_ref, cells_ref) = refs[:count], refs[count:]
    place = lax.axis_index("frame")
    rows = pieces[0].shape[0]
    for mask, piece in enumerate(pieces):
        at = pl.multiple_of((place ^ mask) * rows, rows)
        cells_ref[pl.ds(at, rows)] = piece[...]
    tokens, share = mixed_ref.shape
    packed = lax.dot_general(
        cells_ref[...],
        weight[pl.ds(0, 3 * share)],
        (((1,), (1,)), ((), ())),
        preferred_element_type=jnp.float32,
    ).astype(jnp.bfloat16)
    query = jnp.maximum(packed[:, :share], 0)
    keys = jnp.maximum(packed[:, share : 2 * share], 0)
    values = packed[:, 2 * share :]
    joined = jnp.concatenate([values, jnp.ones_like(values)], axis=1)
    table = lax.dot_general(
        keys, joined, (((0,), (0,)), ((), ())), preferred_element_type=jnp.float32
    ) * (1.0 / tokens)
    head_in = lax.broadcasted_iota(jnp.int32, table.shape, 0) // HEAD
    head_out = lax.rem(lax.broadcasted_iota(jnp.int32, table.shape, 1), share) // HEAD
    table = jnp.where(head_in == head_out, table, 0.0)
    high = table.astype(jnp.bfloat16)
    low = (table - high.astype(jnp.float32)).astype(jnp.bfloat16)
    both = jnp.dot(query, high, preferred_element_type=jnp.float32) + jnp.dot(
        query, low, preferred_element_type=jnp.float32
    )
    mixed_ref[...] = (both[:, :share] / jnp.maximum(both[:, share:], 1.0)).astype(jnp.bfloat16)


def mlp_body(count, columns, *refs):
    mixed, out_weight = refs[:count], refs[count : 2 * count - 1]
    cells, weights, in_parts, scales, kept_ref, sent_ref, first_ref, field = refs[2 * count - 1 :]
    place = lax.axis_index("frame")
    tokens, width = cells.shape
    units = field.shape[1]
    share = mixed[0].shape[1]
    own_out, down = weights[pl.ds(3 * share, share)], weights[pl.ds(4 * share, units)]
    height = tokens // columns
    attn_out = sum(
        jnp.dot(a[...], b, preferred_element_type=jnp.float32)
        for a, b in zip(mixed, [own_out] + [piece[...] for piece in out_weight])
    )
    first = (cells[...].astype(jnp.float32) + norm_rows(attn_out, scales[18:19])).astype(jnp.bfloat16)
    column = lax.rem(lax.broadcasted_iota(jnp.int32, (tokens, units), 0), columns)
    blank = jnp.zeros((columns, units), jnp.float32)
    spread = []
    for part in range(2):
        inner = silu(jnp.dot(first, in_parts[part], preferred_element_type=jnp.float32))
        field[pl.ds(0, columns)] = blank
        field[pl.ds(columns, tokens)] = inner.astype(jnp.bfloat16).astype(jnp.float32)
        field[pl.ds(columns + tokens, columns)] = blank
        sides = []
        for shift_col in range(3):
            sides.append(
                sum(
                    field[pl.ds(shift_row * columns, tokens)]
                    * scales[tap : tap + 1]
                    for shift_row, tap in enumerate(range(2 * shift_col + part, 18, 6))
                )
            )
        spread.append(
            jnp.where(column > 0, pltpu.roll(sides[0], 1, 0), 0.0)
            + sides[1]
            + jnp.where(column < columns - 1, pltpu.roll(sides[2], tokens - 1, 0), 0.0)
        )
    gated = (spread[0] * silu(spread[1])).astype(jnp.bfloat16)
    partial = jnp.dot(gated, down, preferred_element_type=jnp.float32)
    partial = partial.reshape(height // 2, 2, columns, width)
    first = first.reshape(height // 2, 2, columns, width)
    odd = half_of(place) == 1
    kept_ref[...] = jnp.where(odd, partial[:, 1], partial[:, 0])
    sent_ref[...] = jnp.where(odd, partial[:, 0], partial[:, 1])
    first_ref[...] = jnp.where(odd, first[:, 1], first[:, 0])


def norm_body(far_count, step, *refs):
    total, first, gain = refs[:3]
    far, outs, framed = refs[3 : 3 + far_count], refs[3 + far_count : -1], refs[-1]
    level = lax.axis_index("row")
    mlp_out = total[...]
    for piece in far:
        mlp_out = mlp_out + piece[...].astype(jnp.float32)
    second = first[...].astype(jnp.float32) + norm_rows(mlp_out, gain[19:20].reshape(1, 1, -1))
    rows = second.shape[0]
    blank = jnp.zeros(framed.shape[1:], framed.dtype)
    framed[0] = blank
    framed[rows + 1] = blank
    framed[1 : rows + 1] = second.astype(jnp.bfloat16)
    for mask, out in enumerate(outs):
        out[...] = framed[pl.ds(lax.rem(level + mask, len(outs)) * step, step + 2)]


def conv_taps(field, kernel, lane=0, total=0.0):
    frames, rows = field.shape[0] - 2, field.shape[1] - 2
    columns, width = field.shape[2:]
    share = kernel.shape[3]
    tokens = frames * rows * columns
    for shift_time in range(3):
        for shift_row in range(3):
            slab = field[shift_time : shift_time + frames, shift_row : shift_row + rows]
            total = total + lax.dot_general(
                slab.reshape(tokens, width),
                kernel[shift_time, shift_row, :, :, pl.ds(lane, width)].reshape(3 * share, width),
                (((1,), (1,)), ((), ())),
                preferred_element_type=jnp.float32,
            )
    return total


def conv_join(total, columns):
    tokens, share = total.shape[0], total.shape[1] // 3
    column = lax.rem(lax.broadcasted_iota(jnp.int32, (tokens, share), 0), columns)
    before = jnp.where(column > 0, pltpu.roll(total[:, :share], 1, 0), 0.0)
    after = jnp.where(column < columns - 1, pltpu.roll(total[:, 2 * share :], tokens - 1, 0), 0.0)
    return before + total[:, share : 2 * share] + after


def clear_ends(field):
    edge = jnp.zeros(field.shape[1:], field.dtype)
    field[0] = edge
    field[field.shape[0] - 1] = edge


def first_conv_body(height, *refs):
    kernel, hidden_ref, part_ref, field = refs[-4:]
    pieces = refs[:-4]
    count = len(pieces) // 2
    level, place = lax.axis_index("row"), lax.axis_index("frame")
    clear_ends(field)
    for index, piece in enumerate(pieces):
        frame = lax.rem(level + count - index % count, count) + 1
        parity = half_of(place) ^ (index // count)
        for row in range(piece.shape[0]):
            field[frame, 2 * row + parity] = piece[row]
    frames, band, columns, share = hidden_ref.shape
    rows = band - 2
    activated = silu(conv_join(conv_taps(field, kernel), columns).reshape(hidden_ref.shape))
    global_row = level * rows - 1 + lax.broadcasted_iota(jnp.int32, activated.shape, 1)
    inside = (global_row >= 0) & (global_row < height)
    hidden_ref[...] = jnp.where(inside, activated, 0.0).astype(jnp.bfloat16)
    at = pl.multiple_of(place * share, share)
    part_ref[...] = field[1 : frames + 1, 2 : 2 + rows, :, pl.ds(at, share)]


def chip_taps(pieces, chip, kernel, field, total=0.0):
    share = pieces[0].shape[3]
    core = lax.axis_index("frame") % 2
    clear_ends(field)
    for other, piece in enumerate(pieces):
        at = pl.multiple_of((core ^ other) * share, share)
        field[1 : 1 + piece.shape[0], :, :, pl.ds(at, share)] = piece[...]
    return conv_taps(field, kernel, pl.multiple_of(chip * 2 * share, 2 * share), total)


def near_conv_body(own, other, kernel, total_ref, field):
    total_ref[...] = chip_taps([own, other], lax.axis_index("frame") // 2, kernel, field)


def second_conv_body(far, *refs):
    pieces = refs[:far]
    total, part, kernel = refs[far : far + 3]
    outs, field, final = refs[far + 3 : -2], refs[-2], refs[-1]
    place = lax.axis_index("frame")
    result = total[...]
    for index in range(0, far, 2):
        pair = [pieces[index], pieces[index + 1]]
        result = chip_taps(pair, (place // 2) ^ (index // 2 + 1), kernel, field, result)
    result = conv_join(result, part.shape[2]).reshape(part.shape)
    final[...] = part[...].astype(jnp.float32) + result
    lines = final.shape[0] * final.shape[1]
    strip = outs[0].shape[0] // lines
    for mask, out in enumerate(outs):
        at = pl.multiple_of(lax.rem(place + mask, len(outs)) * strip, strip)
        out[...] = jnp.concatenate(
            [
                final[line // final.shape[1], line % final.shape[1], pl.ds(at, strip)]
                for line in range(lines)
            ],
            axis=0,
        ).astype(jnp.bfloat16)


def join_body(*refs):
    pieces, out_ref = refs[:-1], refs[-1]
    place = lax.axis_index("frame")
    share = pieces[0].shape[1]
    frames, rows, strip = out_ref.shape[:3]
    for mask, piece in enumerate(pieces):
        at = pl.multiple_of(lax.rem(place + len(pieces) - mask, len(pieces)) * share, share)
        cells = piece[...].astype(jnp.float32)
        for line in range(frames * rows):
            out_ref[line // rows, line % rows, :, pl.ds(at, share)] = cells[
                line * strip : (line + 1) * strip
            ].astype(jnp.bfloat16)


def by_frames(
    latent,
    qkv_weight,
    out_weight,
    attn_gain,
    in_weight,
    depth_weight,
    down_weight,
    mlp_gain,
    conv_first,
    conv_second,
):
    count = lax.axis_size("frame")
    place = lax.axis_index("frame")
    rows, columns, width = latent.shape[1:]
    height = rows * count
    tokens = height * columns
    share = qkv_weight.shape[1]
    units = down_weight.shape[0]
    half = height // 2
    bf16, f32 = jnp.bfloat16, jnp.float32
    own = latent.reshape(rows * columns, width)
    pieces = [None] * count
    masks = [*range(3, count, 2), 1]
    for mask in masks:
        pairs = [
            (z * count + f, f * count + (z ^ mask)) for z in range(count) for f in range(count)
        ]
        pieces[mask] = lax.ppermute(own, ("row", "frame"), pairs)
    weights = jnp.concatenate([qkv_weight.reshape(3 * share, width), out_weight, down_weight])
    in_parts = jnp.transpose(in_weight, (1, 0, 2))
    *arrived, weights = lax.optimization_barrier((*[pieces[mask] for mask in masks], weights))
    for mask, piece in zip(masks, arrived):
        pieces[mask], pieces[mask ^ 1] = piece, swap(piece, 1)
    out_pieces = gathered_by_mask(out_weight)
    taps = lax.dynamic_slice_in_dim(depth_weight, place * units, units, 3)
    scales = jnp.concatenate([taps.reshape(-1, units), attn_gain[None], mlp_gain[None]])
    mixed, cells = call(
        functools.partial(attend_body, count),
        [*pieces, weights],
        [((tokens, share), bf16), ((tokens, width), bf16)],
        flops=2 * tokens * width * 3 * share,
    )
    kept, sent, first = call(
        functools.partial(mlp_body, count, columns),
        [
            *gathered_by_mask(mixed),
            *out_pieces[1:],
            cells,
            weights,
            in_parts,
            scales,
        ],
        [((half, columns, width), f32)] * 2 + [((half, columns, width), bf16)],
        scratch=[((tokens + 2 * columns, units), f32)],
        flops=2 * tokens * width * (width + 3 * units),
        room=8,
    )
    total = kept + swap(sent, 1)
    far = [swap(total.astype(bf16), mask) for mask in range(3, count, 2)]
    step = rows // 2
    windows = call(
        functools.partial(norm_body, len(far), step),
        [total, first, scales, *far],
        [((step + 2, columns, width), bf16)] * count,
        scratch=[((half + 2, columns, width), bf16)],
        flops=8 * total.size,
    )
    windows = list(windows)
    for mask in (1, 2, 3):
        pairs = [(i, (i + mask) % count) for i in range(count)]
        windows[mask] = lax.ppermute(windows[mask], "row", pairs)
    others = [swap(window, 1) for window in windows]
    hidden, own_part = call(
        functools.partial(first_conv_body, height),
        [*windows, *others, conv_first],
        [((count, rows + 2, columns, share), bf16), ((count, rows, columns, share), bf16)],
        scratch=[((count + 2, rows + 4, columns, width), bf16)],
        flops=2 * count * (rows + 2) * columns * 27 * width * share,
        room=8,
    )
    strip = columns // count
    pieces = gathered_by_mask(hidden)
    taps_shape = (count * rows * columns, 3 * share)
    field = ((count + 2, rows + 2, columns, 2 * share), bf16)
    flops = 2 * count * rows * columns * 27 * 2 * share * share
    (total,) = call(
        near_conv_body,
        [*pieces[:2], conv_second],
        [(taps_shape, f32)],
        scratch=[field],
        flops=flops,
        room=8,
    )
    strips = call(
        functools.partial(second_conv_body, count - 2),
        [*pieces[2:], total, own_part, conv_second],
        [((count * rows * strip, share), bf16)] * count,
        scratch=[field, ((count, rows, columns, share), f32)],
        flops=flops * (count // 2 - 1),
        room=8,
    )
    outs = list(strips)
    for mask in (2, 1, 3):
        pairs = [(i, (i + mask) % count) for i in range(count)]
        outs[mask] = lax.ppermute(strips[mask], "frame", pairs)
    (decoded,) = call(join_body, outs, [((count, rows, strip, width), bf16)])
    return decoded


def solution(mesh):
    body = by_frames if mesh.shape["row"] == mesh.shape["frame"] else local
    in_specs = (
        P(("parts", "frame"), "row", None, None),
        P(None, "frame", None),
        P("frame", None),
        P(),
        P(None, None, "frame"),
        P(),
        P("frame", None),
        P(),
        P(None, None, None, "frame", None),
        P(None, None, None, "frame", None),
    )
    out_specs = P("parts", "row", "frame", None)
    return jax.shard_map(body, mesh=mesh, in_specs=in_specs, out_specs=out_specs, check_vma=False)
```

```python
import functools

import jax
import jax.numpy as jnp
from jax import lax
from jax.experimental import pallas as pl
from jax.experimental.pallas import tpu as pltpu
from jax.sharding import PartitionSpec as P

HEAD = 32


def padded_2(cells, sides, width):
    for axis, dim in sides:
        count = lax.axis_size(axis)
        ends = count - 1
        head = lax.slice_in_dim(cells, 0, width, axis=dim)
        tail = lax.slice_in_dim(cells, cells.shape[dim] - width, cells.shape[dim], axis=dim)
        cells = jnp.concatenate(
            [
                lax.ppermute(tail, axis, [(i, (i + 1) % count) for i in range(ends)]),
                cells,
                lax.ppermute(head, axis, [((i + 1) % count, i) for i in range(ends)]),
            ],
            axis=dim,
        )
    return cells


def norm_rows(values, gain):
    return values * lax.rsqrt(jnp.mean(values * values, axis=-1, keepdims=True) + 1e-05) * gain


def attend(packed):
    frames, height, columns = (packed.shape[0], packed.shape[1], packed.shape[2])
    width = packed.shape[4]
    heads = width // HEAD
    flat = packed.reshape(frames, height * columns, 3, heads, HEAD)
    query = jnp.maximum(flat[:, :, 0], 0)
    keys = jnp.maximum(flat[:, :, 1], 0)
    values = flat[:, :, 2]
    state = jnp.einsum("fnhd,fnhe->fhde", keys, values, preferred_element_type=jnp.float32)
    key_total = jnp.sum(keys.astype(jnp.float32), axis=1)
    state, key_total = (
        lax.psum(state.astype(jnp.bfloat16), "row").astype(jnp.float32),
        lax.psum(key_total.astype(jnp.bfloat16), "row").astype(jnp.float32),
    )
    count = height * lax.axis_size("row") * columns
    state = state / count
    key_mean = key_total / count
    query_wide = query.astype(jnp.float32)
    numer = jnp.einsum("fnhd,fhde->fnhe", query_wide, state, precision=lax.Precision.HIGHEST)
    denom = jnp.maximum(
        jnp.einsum("fnhd,fhd->fnh", query_wide, key_mean, precision=lax.Precision.HIGHEST), 1.0
    )
    return (numer / denom[..., None]).astype(jnp.bfloat16).reshape(frames, height, columns, width)


def depth_mix(inner, depth_local):
    height, columns = (inner.shape[1], inner.shape[2])
    extended = padded_2(inner, (("row", 1),), 1)
    padded = jnp.pad(extended, ((0, 0), (0, 0), (1, 1), (0, 0), (0, 0)))
    spread = jnp.zeros(inner.shape, jnp.float32)
    for shift_row in range(3):
        for shift_col in range(3):
            spread = (
                spread
                + padded[:, shift_row : shift_row + height, shift_col : shift_col + columns].astype(
                    jnp.float32
                )
                * depth_local[shift_row, shift_col]
            )
    return (spread[..., 0, :] * jax.nn.silu(spread[..., 1, :])).astype(jnp.bfloat16)


def conv_tile(extended, kernel):
    frames, padded_rows, columns, width = extended.shape
    height = padded_rows - 2
    out_width = kernel.shape[3]
    padded = jnp.pad(extended, ((1, 1), (0, 0), (1, 1), (0, 0)))
    result = jnp.zeros((frames * height * columns, out_width), jnp.float32)
    for shift_time in range(3):
        for shift_row in range(3):
            slab = padded[shift_time : shift_time + frames, shift_row : shift_row + height]
            stacked = jnp.stack(
                [slab[:, :, shift_col : shift_col + columns] for shift_col in range(3)], axis=3
            )
            result = result + jnp.einsum(
                "nci,coi->no",
                stacked.reshape(-1, 3, width),
                kernel[shift_time, shift_row],
                preferred_element_type=jnp.float32,
            )
    return result.reshape(frames, height, columns, out_width)


def local(
    latent,
    qkv_weight,
    out_weight,
    attn_gain,
    in_weight,
    depth_weight,
    down_weight,
    mlp_gain,
    conv_first,
    conv_second,
):
    frames, height, columns, width = latent.shape
    place = lax.axis_index("frame")
    packed = jnp.einsum(
        "frwc,kjc->frwkj",
        latent,
        lax.all_gather(qkv_weight, "frame", axis=1, tiled=True),
        preferred_element_type=jnp.float32,
    ).astype(jnp.bfloat16)
    mixed = attend(packed)
    section = mixed
    attn_out = jnp.einsum(
        "frwj,jc->frwc",
        section,
        lax.all_gather(out_weight, "frame", axis=0, tiled=True),
        preferred_element_type=jnp.float32,
    )
    first = (latent.astype(jnp.float32) + norm_rows(attn_out, attn_gain)).astype(jnp.bfloat16)
    inner = jax.nn.silu(
        jnp.einsum(
            "frwc,ckj->frwkj",
            first,
            lax.all_gather(in_weight, "frame", axis=2, tiled=True),
            preferred_element_type=jnp.float32,
        )
    ).astype(jnp.bfloat16)
    gated = depth_mix(inner, depth_weight)
    section = gated
    mlp_out = jnp.einsum(
        "frwj,jc->frwc",
        section,
        lax.all_gather(down_weight, "frame", axis=0, tiled=True),
        preferred_element_type=jnp.float32,
    )
    second = (first.astype(jnp.float32) + norm_rows(mlp_out, mlp_gain)).astype(jnp.bfloat16)
    gathered = lax.all_gather(second, "frame", axis=0, tiled=True)
    out_share = conv_first.shape[3]
    extended = padded_2(gathered, (("row", 1),), 2)
    activated = jax.nn.silu(conv_tile(extended, conv_first))
    global_row = lax.axis_index("row") * height - 1 + lax.iota(jnp.int32, height + 2)
    inside = ((global_row >= 0) & (global_row < height * lax.axis_size("row"))).astype(jnp.float32)
    hidden_conv = (activated * inside[None, :, None, None]).astype(jnp.bfloat16)
    joined = lax.all_gather(hidden_conv, "frame", axis=3, tiled=True)
    result = conv_tile(joined, conv_second)
    own_part = lax.dynamic_slice_in_dim(gathered, place * out_share, out_share, 3)
    final = (own_part.astype(jnp.float32) + result).astype(jnp.bfloat16)
    return lax.all_to_all(final, "frame", split_axis=2, concat_axis=3, tiled=True)


def swap(cells, mask):
    count = lax.axis_size("frame")
    return lax.ppermute(cells, "frame", [(i, i ^ mask) for i in range(count)])


def in_order(pieces, place, dim):
    step = 1
    while step < len(pieces):
        flip = (place & step) != 0
        pieces = [jnp.where(flip, pieces[i ^ step], pieces[i]) for i in range(len(pieces))]
        step *= 2
    return jnp.concatenate(pieces, axis=dim)


def gathered_by_mask(cells):
    count = lax.axis_size("frame")
    pieces = [None] * count
    pieces[0] = cells
    masks = list(range(3, count, 2))
    for mask in masks:
        pieces[mask] = swap(cells, mask)
    for mask in [0] + masks:
        pieces[mask ^ 1] = swap(pieces[mask], 1)
    return pieces


def silu(values):
    return values / (1.0 + jnp.exp(-values))


def half_of(place):
    return (place ^ (place >> 1)) & 1


def call(body, operands, outs, scratch=(), flops=0, room=4):
    moved = sum(o.size * o.dtype.itemsize for o in operands)
    return pl.pallas_call(
        body,
        out_shape=[jax.ShapeDtypeStruct(shape, kind) for shape, kind in outs],
        scratch_shapes=[pltpu.VMEM(shape, kind) for shape, kind in scratch],
        compiler_params=pltpu.CompilerParams(vmem_limit_bytes=room * 1024 * 1024),
        cost_estimate=pl.CostEstimate(flops=flops, bytes_accessed=moved, transcendentals=0),
    )(*operands)


def attend_body(count, *refs):
    pieces, (weight, mixed_ref, cells_ref) = refs[:count], refs[count:]
    place = lax.axis_index("frame")
    rows = pieces[0].shape[0]
    for mask, piece in enumerate(pieces):
        at = pl.multiple_of((place ^ mask) * rows, rows)
        cells_ref[pl.ds(at, rows)] = piece[...]
    tokens, share = mixed_ref.shape
    packed = lax.dot_general(
        cells_ref[...],
        weight[pl.ds(0, 3 * share)],
        (((1,), (1,)), ((), ())),
        preferred_element_type=jnp.float32,
    ).astype(jnp.bfloat16)
    query = jnp.maximum(packed[:, :share], 0)
    keys = jnp.maximum(packed[:, share : 2 * share], 0)
    values = packed[:, 2 * share :]
    joined = jnp.concatenate([values, jnp.ones_like(values)], axis=1)
    table = lax.dot_general(
        keys, joined, (((0,), (0,)), ((), ())), preferred_element_type=jnp.float32
    ) * (1.0 / tokens)
    head_in = lax.broadcasted_iota(jnp.int32, table.shape, 0) // HEAD
    head_out = lax.rem(lax.broadcasted_iota(jnp.int32, table.shape, 1), share) // HEAD
    table = jnp.where(head_in == head_out, table, 0.0)
    high = table.astype(jnp.bfloat16)
    low = (table - high.astype(jnp.float32)).astype(jnp.bfloat16)
    both = jnp.dot(
        jnp.concatenate([query, query], axis=1),
        jnp.concatenate([high, low], axis=0),
        preferred_element_type=jnp.float32,
    )
    mixed_ref[...] = (both[:, :share] / jnp.maximum(both[:, share:], 1.0)).astype(jnp.bfloat16)


def mlp_body(count, columns, *refs):
    mixed, out_weight = refs[:count], refs[count : 2 * count - 1]
    cells, weights, in_parts, scales, kept_ref, sent_ref, first_ref, field = refs[2 * count - 1 :]
    place = lax.axis_index("frame")
    tokens, width = cells.shape
    units = field.shape[1]
    share = mixed[0].shape[1]
    own_out, down = weights[pl.ds(3 * share, share)], weights[pl.ds(4 * share, units)]
    height = tokens // columns
    attn_out = jnp.dot(
        jnp.concatenate([piece[...] for piece in mixed], axis=1),
        jnp.concatenate([own_out] + [piece[...] for piece in out_weight], axis=0),
        preferred_element_type=jnp.float32,
    )
    first = (cells[...].astype(jnp.float32) + norm_rows(attn_out, scales[18:19])).astype(jnp.bfloat16)
    column = lax.rem(lax.broadcasted_iota(jnp.int32, (tokens, units), 0), columns)
    blank = jnp.zeros((columns, units), jnp.float32)
    spread = []
    for part in range(2):
        inner = silu(jnp.dot(first, in_parts[part], preferred_element_type=jnp.float32))
        field[pl.ds(0, columns)] = blank
        field[pl.ds(columns, tokens)] = inner.astype(jnp.bfloat16).astype(jnp.float32)
        field[pl.ds(columns + tokens, columns)] = blank
        sides = []
        for shift_col in range(3):
            sides.append(
                sum(
                    field[pl.ds(shift_row * columns, tokens)]
                    * scales[tap : tap + 1]
                    for shift_row, tap in enumerate(range(2 * shift_col + part, 18, 6))
                )
            )
        spread.append(
            jnp.where(column > 0, pltpu.roll(sides[0], 1, 0), 0.0)
            + sides[1]
            + jnp.where(column < columns - 1, pltpu.roll(sides[2], tokens - 1, 0), 0.0)
        )
    gated = (spread[0] * silu(spread[1])).astype(jnp.bfloat16)
    partial = jnp.dot(gated, down, preferred_element_type=jnp.float32)
    partial = partial.reshape(height // 2, 2, columns, width)
    first = first.reshape(height // 2, 2, columns, width)
    odd = half_of(place) == 1
    kept_ref[...] = jnp.where(odd, partial[:, 1], partial[:, 0])
    sent_ref[...] = jnp.where(odd, partial[:, 0], partial[:, 1])
    first_ref[...] = jnp.where(odd, first[:, 1], first[:, 0])


def norm_body(far_count, step, *refs):
    total, first, gain = refs[:3]
    far, outs, framed = refs[3 : 3 + far_count], refs[3 + far_count : -1], refs[-1]
    level = lax.axis_index("row")
    mlp_out = total[...]
    for piece in far:
        mlp_out = mlp_out + piece[...].astype(jnp.float32)
    second = first[...].astype(jnp.float32) + norm_rows(mlp_out, gain[19:20].reshape(1, 1, -1))
    rows = second.shape[0]
    blank = jnp.zeros(framed.shape[1:], framed.dtype)
    framed[0] = blank
    framed[rows + 1] = blank
    framed[1 : rows + 1] = second.astype(jnp.bfloat16)
    for mask, out in enumerate(outs):
        out[...] = framed[pl.ds(lax.rem(level + mask, len(outs)) * step, step + 2)]


def conv_taps(field, kernel, lane=0, total=0.0, upright=True):
    frames, rows = field.shape[0] - 2, field.shape[1] - 2
    columns, width = field.shape[2:]
    share = kernel.shape[3]
    for shift_time in range(3):
        for shift_row in range(3):
            slab = field[shift_time : shift_time + frames, shift_row : shift_row + rows]
            slab = slab.reshape(frames * rows * columns, width)
            taps = kernel[shift_time, shift_row, :, :, pl.ds(lane, width)].reshape(-1, width)
            total = total + lax.dot_general(
                *((slab, taps) if upright else (taps, slab)),
                (((1,), (1,)), ((), ())),
                preferred_element_type=jnp.float32,
            )
    return total


def conv_join(total, columns, upright=True):
    axis = 0 if upright else 1
    left, middle, right = jnp.split(total, 3, axis=1 - axis)
    tokens = left.shape[axis]
    column = lax.rem(lax.broadcasted_iota(jnp.int32, left.shape, axis), columns)
    before = jnp.where(column > 0, pltpu.roll(left, 1, axis), 0.0)
    after = jnp.where(column < columns - 1, pltpu.roll(right, tokens - 1, axis), 0.0)
    result = before + middle + after
    return result if upright else result.T


def clear_ends(field):
    edge = jnp.zeros(field.shape[1:], field.dtype)
    field[0] = edge
    field[field.shape[0] - 1] = edge


def first_conv_body(height, *refs):
    kernel, hidden_ref, part_ref, field = refs[-4:]
    pieces = refs[:-4]
    count = len(pieces) // 2
    level, place = lax.axis_index("row"), lax.axis_index("frame")
    clear_ends(field)
    for index, piece in enumerate(pieces):
        frame = lax.rem(level + count - index % count, count) + 1
        parity = half_of(place) ^ (index // count)
        for row in range(piece.shape[0]):
            field[frame, 2 * row + parity] = piece[row]
    frames, band, columns, share = hidden_ref.shape
    rows = band - 2
    total = conv_taps(field, kernel, upright=False)
    activated = silu(conv_join(total, columns, upright=False).reshape(hidden_ref.shape))
    global_row = level * rows - 1 + lax.broadcasted_iota(jnp.int32, activated.shape, 1)
    inside = (global_row >= 0) & (global_row < height)
    hidden_ref[...] = jnp.where(inside, activated, 0.0).astype(jnp.bfloat16)
    at = pl.multiple_of(place * share, share)
    part_ref[...] = field[1 : frames + 1, 2 : 2 + rows, :, pl.ds(at, share)]


def chip_taps(pieces, chip, kernel, field, total=0.0):
    share = pieces[0].shape[3]
    core = lax.axis_index("frame") % 2
    clear_ends(field)
    for other, piece in enumerate(pieces):
        at = pl.multiple_of((core ^ other) * share, share)
        field[1 : 1 + piece.shape[0], :, :, pl.ds(at, share)] = piece[...]
    return conv_taps(field, kernel, pl.multiple_of(chip * 2 * share, 2 * share), total)


def near_conv_body(own, other, kernel, total_ref, field):
    total_ref[...] = chip_taps([own, other], lax.axis_index("frame") // 2, kernel, field)


def second_conv_body(far, *refs):
    pieces = refs[:far]
    total, part, kernel = refs[far : far + 3]
    outs, field, final = refs[far + 3 : -2], refs[-2], refs[-1]
    place = lax.axis_index("frame")
    result = total[...]
    for index in range(0, far, 2):
        pair = [pieces[index], pieces[index + 1]]
        result = chip_taps(pair, (place // 2) ^ (index // 2 + 1), kernel, field, result)
    result = conv_join(result, part.shape[2]).reshape(part.shape)
    final[...] = part[...].astype(jnp.float32) + result
    lines = final.shape[0] * final.shape[1]
    strip = outs[0].shape[0] // lines
    for mask, out in enumerate(outs):
        at = pl.multiple_of(lax.rem(place + mask, len(outs)) * strip, strip)
        out[...] = jnp.concatenate(
            [
                final[line // final.shape[1], line % final.shape[1], pl.ds(at, strip)]
                for line in range(lines)
            ],
            axis=0,
        ).astype(jnp.bfloat16)


def join_body(*refs):
    pieces, out_ref = refs[:-1], refs[-1]
    place = lax.axis_index("frame")
    share = pieces[0].shape[1]
    frames, rows, strip = out_ref.shape[:3]
    for mask, piece in enumerate(pieces):
        at = pl.multiple_of(lax.rem(place + len(pieces) - mask, len(pieces)) * share, share)
        cells = piece[...].astype(jnp.float32)
        for line in range(frames * rows):
            out_ref[line // rows, line % rows, :, pl.ds(at, share)] = cells[
                line * strip : (line + 1) * strip
            ].astype(jnp.bfloat16)


def by_frames(
    latent,
    qkv_weight,
    out_weight,
    attn_gain,
    in_weight,
    depth_weight,
    down_weight,
    mlp_gain,
    conv_first,
    conv_second,
):
    count = lax.axis_size("frame")
    place = lax.axis_index("frame")
    rows, columns, width = latent.shape[1:]
    height = rows * count
    tokens = height * columns
    share = qkv_weight.shape[1]
    units = down_weight.shape[0]
    half = height // 2
    bf16, f32 = jnp.bfloat16, jnp.float32
    own = latent.reshape(rows * columns, width)
    pieces = [None] * count
    masks = [*range(2, count, 2), 1]
    for mask in masks:
        pairs = [
            (z * count + f, f * count + (z ^ mask)) for z in range(count) for f in range(count)
        ]
        pieces[mask] = lax.ppermute(own, ("row", "frame"), pairs)
    weights = jnp.concatenate([qkv_weight.reshape(3 * share, width), out_weight, down_weight])
    in_parts = jnp.transpose(in_weight, (1, 0, 2))
    *arrived, weights = lax.optimization_barrier((*[pieces[mask] for mask in masks], weights))
    for mask, piece in zip(masks, arrived):
        pieces[mask], pieces[mask ^ 1] = piece, swap(piece, 1)
    out_pieces = gathered_by_mask(out_weight)
    taps = lax.dynamic_slice_in_dim(depth_weight, place * units, units, 3)
    scales = jnp.concatenate([taps.reshape(-1, units), attn_gain[None], mlp_gain[None]])
    mixed, cells = call(
        functools.partial(attend_body, count),
        [*pieces, weights],
        [((tokens, share), bf16), ((tokens, width), bf16)],
        flops=2 * tokens * width * 3 * share,
    )
    kept, sent, first = call(
        functools.partial(mlp_body, count, columns),
        [
            *gathered_by_mask(mixed),
            *out_pieces[1:],
            cells,
            weights,
            in_parts,
            scales,
        ],
        [((half, columns, width), f32)] * 2 + [((half, columns, width), bf16)],
        scratch=[((tokens + 2 * columns, units), f32)],
        flops=2 * tokens * width * (width + 3 * units),
        room=8,
    )
    total = kept + swap(sent, 1)
    far = [swap(total.astype(bf16), mask) for mask in range(3, count, 2)]
    step = rows // 2
    windows = call(
        functools.partial(norm_body, len(far), step),
        [total, first, scales, *far],
        [((step + 2, columns, width), bf16)] * count,
        scratch=[((half + 2, columns, width), bf16)],
        flops=8 * total.size,
    )
    windows = list(windows)
    for mask in range(1, count):
        pairs = [(i, (i + mask) % count) for i in range(count)]
        windows[mask] = lax.ppermute(windows[mask], "row", pairs)
    others = [swap(window, 1) for window in windows]
    hidden, own_part = call(
        functools.partial(first_conv_body, height),
        [*windows, *others, conv_first],
        [((count, rows + 2, columns, share), bf16), ((count, rows, columns, share), bf16)],
        scratch=[((count + 2, rows + 4, columns, width), bf16)],
        flops=2 * count * (rows + 2) * columns * 27 * width * share,
        room=8,
    )
    strip = columns // count
    pieces = gathered_by_mask(hidden)
    taps_shape = (count * rows * columns, 3 * share)
    field = ((count + 2, rows + 2, columns, 2 * share), bf16)
    flops = 2 * count * rows * columns * 27 * 2 * share * share
    (total,) = call(
        near_conv_body,
        [*pieces[:2], conv_second],
        [(taps_shape, f32)],
        scratch=[field],
        flops=flops,
        room=8,
    )
    strips = call(
        functools.partial(second_conv_body, count - 2),
        [*pieces[2:], total, own_part, conv_second],
        [((count * rows * strip, share), bf16)] * count,
        scratch=[field, ((count, rows, columns, share), f32)],
        flops=flops * (count // 2 - 1),
        room=8,
    )
    outs = list(strips)
    for mask in range(1, count):
        pairs = [(i, (i + mask) % count) for i in range(count)]
        outs[mask] = lax.ppermute(strips[mask], "frame", pairs)
    (decoded,) = call(join_body, outs, [((count, rows, strip, width), bf16)])
    return decoded


def solution(mesh):
    count = mesh.shape["frame"]
    square = mesh.shape["row"] == count > 1 and count & (count - 1) == 0
    body = by_frames if square else local
    in_specs = (
        P(("parts", "frame"), "row", None, None),
        P(None, "frame", None),
        P("frame", None),
        P(),
        P(None, None, "frame"),
        P(),
        P("frame", None),
        P(),
        P(None, None, None, "frame", None),
        P(None, None, None, "frame", None),
    )
    out_specs = P("parts", "row", "frame", None)
    return jax.shard_map(body, mesh=mesh, in_specs=in_specs, out_specs=out_specs, check_vma=False)
```

```python
import functools

import jax
import jax.numpy as jnp
from jax import lax
from jax.experimental import pallas as pl
from jax.experimental.pallas import tpu as pltpu
from jax.sharding import PartitionSpec as P

HEAD = 32


def padded_2(cells, sides, width):
    for axis, dim in sides:
        count = lax.axis_size(axis)
        ends = count - 1
        head = lax.slice_in_dim(cells, 0, width, axis=dim)
        tail = lax.slice_in_dim(cells, cells.shape[dim] - width, cells.shape[dim], axis=dim)
        cells = jnp.concatenate(
            [
                lax.ppermute(tail, axis, [(i, (i + 1) % count) for i in range(ends)]),
                cells,
                lax.ppermute(head, axis, [((i + 1) % count, i) for i in range(ends)]),
            ],
            axis=dim,
        )
    return cells


def norm_rows(values, gain):
    return values * lax.rsqrt(jnp.mean(values * values, axis=-1, keepdims=True) + 1e-05) * gain


def attend(packed):
    frames, height, columns = (packed.shape[0], packed.shape[1], packed.shape[2])
    width = packed.shape[4]
    heads = width // HEAD
    flat = packed.reshape(frames, height * columns, 3, heads, HEAD)
    query = jnp.maximum(flat[:, :, 0], 0)
    keys = jnp.maximum(flat[:, :, 1], 0)
    values = flat[:, :, 2]
    state = jnp.einsum("fnhd,fnhe->fhde", keys, values, preferred_element_type=jnp.float32)
    key_total = jnp.sum(keys.astype(jnp.float32), axis=1)
    state, key_total = (
        lax.psum(state.astype(jnp.bfloat16), "row").astype(jnp.float32),
        lax.psum(key_total.astype(jnp.bfloat16), "row").astype(jnp.float32),
    )
    count = height * lax.axis_size("row") * columns
    state = state / count
    key_mean = key_total / count
    query_wide = query.astype(jnp.float32)
    numer = jnp.einsum("fnhd,fhde->fnhe", query_wide, state, precision=lax.Precision.HIGHEST)
    denom = jnp.maximum(
        jnp.einsum("fnhd,fhd->fnh", query_wide, key_mean, precision=lax.Precision.HIGHEST), 1.0
    )
    return (numer / denom[..., None]).astype(jnp.bfloat16).reshape(frames, height, columns, width)


def depth_mix(inner, depth_local):
    height, columns = (inner.shape[1], inner.shape[2])
    extended = padded_2(inner, (("row", 1),), 1)
    padded = jnp.pad(extended, ((0, 0), (0, 0), (1, 1), (0, 0), (0, 0)))
    spread = jnp.zeros(inner.shape, jnp.float32)
    for shift_row in range(3):
        for shift_col in range(3):
            spread = (
                spread
                + padded[:, shift_row : shift_row + height, shift_col : shift_col + columns].astype(
                    jnp.float32
                )
                * depth_local[shift_row, shift_col]
            )
    return (spread[..., 0, :] * jax.nn.silu(spread[..., 1, :])).astype(jnp.bfloat16)


def conv_tile(extended, kernel):
    frames, padded_rows, columns, width = extended.shape
    height = padded_rows - 2
    out_width = kernel.shape[3]
    padded = jnp.pad(extended, ((1, 1), (0, 0), (1, 1), (0, 0)))
    result = jnp.zeros((frames * height * columns, out_width), jnp.float32)
    for shift_time in range(3):
        for shift_row in range(3):
            slab = padded[shift_time : shift_time + frames, shift_row : shift_row + height]
            stacked = jnp.stack(
                [slab[:, :, shift_col : shift_col + columns] for shift_col in range(3)], axis=3
            )
            result = result + jnp.einsum(
                "nci,coi->no",
                stacked.reshape(-1, 3, width),
                kernel[shift_time, shift_row],
                preferred_element_type=jnp.float32,
            )
    return result.reshape(frames, height, columns, out_width)


def local(
    latent,
    qkv_weight,
    out_weight,
    attn_gain,
    in_weight,
    depth_weight,
    down_weight,
    mlp_gain,
    conv_first,
    conv_second,
):
    frames, height, columns, width = latent.shape
    place = lax.axis_index("frame")
    packed = jnp.einsum(
        "frwc,kjc->frwkj",
        latent,
        lax.all_gather(qkv_weight, "frame", axis=1, tiled=True),
        preferred_element_type=jnp.float32,
    ).astype(jnp.bfloat16)
    mixed = attend(packed)
    section = mixed
    attn_out = jnp.einsum(
        "frwj,jc->frwc",
        section,
        lax.all_gather(out_weight, "frame", axis=0, tiled=True),
        preferred_element_type=jnp.float32,
    )
    first = (latent.astype(jnp.float32) + norm_rows(attn_out, attn_gain)).astype(jnp.bfloat16)
    inner = jax.nn.silu(
        jnp.einsum(
            "frwc,ckj->frwkj",
            first,
            lax.all_gather(in_weight, "frame", axis=2, tiled=True),
            preferred_element_type=jnp.float32,
        )
    ).astype(jnp.bfloat16)
    gated = depth_mix(inner, depth_weight)
    section = gated
    mlp_out = jnp.einsum(
        "frwj,jc->frwc",
        section,
        lax.all_gather(down_weight, "frame", axis=0, tiled=True),
        preferred_element_type=jnp.float32,
    )
    second = (first.astype(jnp.float32) + norm_rows(mlp_out, mlp_gain)).astype(jnp.bfloat16)
    gathered = lax.all_gather(second, "frame", axis=0, tiled=True)
    out_share = conv_first.shape[3]
    extended = padded_2(gathered, (("row", 1),), 2)
    activated = jax.nn.silu(conv_tile(extended, conv_first))
    global_row = lax.axis_index("row") * height - 1 + lax.iota(jnp.int32, height + 2)
    inside = ((global_row >= 0) & (global_row < height * lax.axis_size("row"))).astype(jnp.float32)
    hidden_conv = (activated * inside[None, :, None, None]).astype(jnp.bfloat16)
    joined = lax.all_gather(hidden_conv, "frame", axis=3, tiled=True)
    result = conv_tile(joined, conv_second)
    own_part = lax.dynamic_slice_in_dim(gathered, place * out_share, out_share, 3)
    final = (own_part.astype(jnp.float32) + result).astype(jnp.bfloat16)
    return lax.all_to_all(final, "frame", split_axis=2, concat_axis=3, tiled=True)


def swap(cells, mask):
    count = lax.axis_size("frame")
    return lax.ppermute(cells, "frame", [(i, i ^ mask) for i in range(count)])


def in_order(pieces, place, dim):
    step = 1
    while step < len(pieces):
        flip = (place & step) != 0
        pieces = [jnp.where(flip, pieces[i ^ step], pieces[i]) for i in range(len(pieces))]
        step *= 2
    return jnp.concatenate(pieces, axis=dim)


def gathered_by_mask(cells):
    count = lax.axis_size("frame")
    pieces = [None] * count
    pieces[0] = cells
    masks = list(range(3, count, 2))
    for mask in masks:
        pieces[mask] = swap(cells, mask)
    for mask in [0] + masks:
        pieces[mask ^ 1] = swap(pieces[mask], 1)
    return pieces


def silu(values):
    return values / (1.0 + jnp.exp(-values))


def half_of(place):
    return (place ^ (place >> 1)) & 1


def call(body, operands, outs, scratch=(), flops=0, room=4):
    moved = sum(o.size * o.dtype.itemsize for o in operands)
    return pl.pallas_call(
        body,
        out_shape=[jax.ShapeDtypeStruct(shape, kind) for shape, kind in outs],
        scratch_shapes=[pltpu.VMEM(shape, kind) for shape, kind in scratch],
        compiler_params=pltpu.CompilerParams(vmem_limit_bytes=room * 1024 * 1024),
        cost_estimate=pl.CostEstimate(flops=flops, bytes_accessed=moved, transcendentals=0),
    )(*operands)


def attend_body(count, *refs):
    pieces, (weight, mixed_ref, cells_ref) = refs[:count], refs[count:]
    place = lax.axis_index("frame")
    rows = pieces[0].shape[0]
    for mask, piece in enumerate(pieces):
        at = pl.multiple_of((place ^ mask) * rows, rows)
        cells_ref[pl.ds(at, rows)] = piece[...]
    tokens, share = mixed_ref.shape
    packed = lax.dot_general(
        cells_ref[...],
        weight[pl.ds(0, 3 * share)],
        (((1,), (1,)), ((), ())),
        preferred_element_type=jnp.float32,
    ).astype(jnp.bfloat16)
    query = jnp.maximum(packed[:, :share], 0)
    keys = jnp.maximum(packed[:, share : 2 * share], 0)
    values = packed[:, 2 * share :]
    joined = jnp.concatenate([values, jnp.ones_like(values)], axis=1)
    table = lax.dot_general(
        keys, joined, (((0,), (0,)), ((), ())), preferred_element_type=jnp.float32
    ) * (1.0 / tokens)
    head_in = lax.broadcasted_iota(jnp.int32, table.shape, 0) // HEAD
    head_out = lax.rem(lax.broadcasted_iota(jnp.int32, table.shape, 1), share) // HEAD
    table = jnp.where(head_in == head_out, table, 0.0)
    high = table.astype(jnp.bfloat16)
    low = (table - high.astype(jnp.float32)).astype(jnp.bfloat16)
    both = jnp.dot(
        jnp.concatenate([query, query], axis=1),
        jnp.concatenate([high, low], axis=0),
        preferred_element_type=jnp.float32,
    )
    mixed_ref[...] = (both[:, :share] / jnp.maximum(both[:, share:], 1.0)).astype(jnp.bfloat16)


def mlp_body(count, columns, *refs):
    mixed, out_weight = refs[:count], refs[count : 2 * count - 1]
    cells, weights, in_parts, scales, kept_ref, sent_ref, first_ref, field = refs[2 * count - 1 :]
    place = lax.axis_index("frame")
    tokens, width = cells.shape
    units = field.shape[1]
    share = mixed[0].shape[1]
    own_out, down = weights[pl.ds(3 * share, share)], weights[pl.ds(4 * share, units)]
    height = tokens // columns
    attn_out = jnp.dot(
        jnp.concatenate([piece[...] for piece in mixed], axis=1),
        jnp.concatenate([own_out] + [piece[...] for piece in out_weight], axis=0),
        preferred_element_type=jnp.float32,
    )
    first = (cells[...].astype(jnp.float32) + norm_rows(attn_out, scales[18:19])).astype(jnp.bfloat16)
    column = lax.rem(lax.broadcasted_iota(jnp.int32, (tokens, units), 0), columns)
    blank = jnp.zeros((columns, units), jnp.float32)
    spread = []
    for part in range(2):
        inner = silu(jnp.dot(first, in_parts[part], preferred_element_type=jnp.float32))
        field[pl.ds(0, columns)] = blank
        field[pl.ds(columns, tokens)] = inner.astype(jnp.bfloat16).astype(jnp.float32)
        field[pl.ds(columns + tokens, columns)] = blank
        sides = []
        for shift_col in range(3):
            sides.append(
                sum(
                    field[pl.ds(shift_row * columns, tokens)]
                    * scales[tap : tap + 1]
                    for shift_row, tap in enumerate(range(2 * shift_col + part, 18, 6))
                )
            )
        spread.append(
            jnp.where(column > 0, pltpu.roll(sides[0], 1, 0), 0.0)
            + sides[1]
            + jnp.where(column < columns - 1, pltpu.roll(sides[2], tokens - 1, 0), 0.0)
        )
    gated = (spread[0] * silu(spread[1])).astype(jnp.bfloat16)
    partial = jnp.dot(gated, down, preferred_element_type=jnp.float32)
    partial = partial.reshape(height // 2, 2, columns, width)
    first = first.reshape(height // 2, 2, columns, width)
    odd = half_of(place) == 1
    kept_ref[...] = jnp.where(odd, partial[:, 1], partial[:, 0])
    sent_ref[...] = jnp.where(odd, partial[:, 0], partial[:, 1]).astype(jnp.bfloat16)
    first_ref[...] = jnp.where(odd, first[:, 1], first[:, 0])


def norm_body(far_count, step, *refs):
    total, first, gain = refs[:3]
    far, outs, framed = refs[3 : 3 + far_count], refs[3 + far_count : -1], refs[-1]
    level = lax.axis_index("row")
    mlp_out = total[...]
    for piece in far:
        mlp_out = mlp_out + piece[...].astype(jnp.float32)
    second = first[...].astype(jnp.float32) + norm_rows(mlp_out, gain[19:20].reshape(1, 1, -1))
    rows = second.shape[0]
    blank = jnp.zeros(framed.shape[1:], framed.dtype)
    framed[0] = blank
    framed[rows + 1] = blank
    framed[1 : rows + 1] = second.astype(jnp.bfloat16)
    for mask, out in enumerate(outs):
        out[...] = framed[pl.ds(lax.rem(level + mask, len(outs)) * step, step + 2)]


def conv_taps(field, kernel, lane=0, total=0.0, upright=True):
    frames, rows = field.shape[0] - 2, field.shape[1] - 2
    columns, width = field.shape[2:]
    share = kernel.shape[3]
    for shift_time in range(3):
        for shift_row in range(3):
            slab = field[shift_time : shift_time + frames, shift_row : shift_row + rows]
            slab = slab.reshape(frames * rows * columns, width)
            taps = kernel[shift_time, shift_row, :, :, pl.ds(lane, width)].reshape(-1, width)
            total = total + lax.dot_general(
                *((slab, taps) if upright else (taps, slab)),
                (((1,), (1,)), ((), ())),
                preferred_element_type=jnp.float32,
            )
    return total


def conv_join(total, columns, upright=True):
    axis = 0 if upright else 1
    left, middle, right = jnp.split(total, 3, axis=1 - axis)
    tokens = left.shape[axis]
    column = lax.rem(lax.broadcasted_iota(jnp.int32, left.shape, axis), columns)
    before = jnp.where(column > 0, pltpu.roll(left, 1, axis), 0.0)
    after = jnp.where(column < columns - 1, pltpu.roll(right, tokens - 1, axis), 0.0)
    result = before + middle + after
    return result if upright else result.T


def clear_ends(field):
    edge = jnp.zeros(field.shape[1:], field.dtype)
    field[0] = edge
    field[field.shape[0] - 1] = edge


def first_conv_body(height, *refs):
    kernel, hidden_ref, part_ref, field = refs[-4:]
    pieces = refs[:-4]
    count = len(pieces) // 2
    level, place = lax.axis_index("row"), lax.axis_index("frame")
    clear_ends(field)
    for index, piece in enumerate(pieces):
        frame = lax.rem(level + count - index % count, count) + 1
        parity = half_of(place) ^ (index // count)
        for row in range(piece.shape[0]):
            field[frame, 2 * row + parity] = piece[row]
    frames, band, columns, share = hidden_ref.shape
    rows = band - 2
    total = conv_taps(field, kernel, upright=False)
    activated = silu(conv_join(total, columns, upright=False).reshape(hidden_ref.shape))
    global_row = level * rows - 1 + lax.broadcasted_iota(jnp.int32, activated.shape, 1)
    inside = (global_row >= 0) & (global_row < height)
    hidden_ref[...] = jnp.where(inside, activated, 0.0).astype(jnp.bfloat16)
    at = pl.multiple_of(place * share, share)
    part_ref[...] = field[1 : frames + 1, 2 : 2 + rows, :, pl.ds(at, share)]


def chip_taps(pieces, chip, kernel, field, total=0.0):
    share = pieces[0].shape[3]
    core = lax.axis_index("frame") % 2
    clear_ends(field)
    for other, piece in enumerate(pieces):
        at = pl.multiple_of((core ^ other) * share, share)
        field[1 : 1 + piece.shape[0], :, :, pl.ds(at, share)] = piece[...]
    return conv_taps(field, kernel, pl.multiple_of(chip * 2 * share, 2 * share), total)


def near_conv_body(own, other, kernel, total_ref, field):
    total_ref[...] = chip_taps([own, other], lax.axis_index("frame") // 2, kernel, field)


def second_conv_body(far, *refs):
    pieces = refs[:far]
    total, part, kernel = refs[far : far + 3]
    outs, field, final = refs[far + 3 : -2], refs[-2], refs[-1]
    place = lax.axis_index("frame")
    result = total[...]
    for index in range(0, far, 2):
        pair = [pieces[index], pieces[index + 1]]
        result = chip_taps(pair, (place // 2) ^ (index // 2 + 1), kernel, field, result)
    result = conv_join(result, part.shape[2]).reshape(part.shape)
    final[...] = part[...].astype(jnp.float32) + result
    lines = final.shape[0] * final.shape[1]
    strip = outs[0].shape[0] // lines
    for mask, out in enumerate(outs):
        at = pl.multiple_of(lax.rem(place + mask, len(outs)) * strip, strip)
        out[...] = jnp.concatenate(
            [
                final[line // final.shape[1], line % final.shape[1], pl.ds(at, strip)]
                for line in range(lines)
            ],
            axis=0,
        ).astype(jnp.bfloat16)


def join_body(*refs):
    pieces, out_ref = refs[:-1], refs[-1]
    place = lax.axis_index("frame")
    share = pieces[0].shape[1]
    frames, rows, strip = out_ref.shape[:3]
    for mask, piece in enumerate(pieces):
        at = pl.multiple_of(lax.rem(place + len(pieces) - mask, len(pieces)) * share, share)
        cells = piece[...].astype(jnp.float32)
        for line in range(frames * rows):
            out_ref[line // rows, line % rows, :, pl.ds(at, share)] = cells[
                line * strip : (line + 1) * strip
            ].astype(jnp.bfloat16)


def by_frames(
    latent,
    qkv_weight,
    out_weight,
    attn_gain,
    in_weight,
    depth_weight,
    down_weight,
    mlp_gain,
    conv_first,
    conv_second,
):
    count = lax.axis_size("frame")
    place = lax.axis_index("frame")
    rows, columns, width = latent.shape[1:]
    height = rows * count
    tokens = height * columns
    share = qkv_weight.shape[1]
    units = down_weight.shape[0]
    half = height // 2
    bf16, f32 = jnp.bfloat16, jnp.float32
    own = latent.reshape(rows * columns, width)
    pieces = [None] * count
    masks = [*range(2, count, 2), 1]
    for mask in masks:
        pairs = [
            (z * count + f, f * count + (z ^ mask)) for z in range(count) for f in range(count)
        ]
        pieces[mask] = lax.ppermute(own, ("row", "frame"), pairs)
    weights = jnp.concatenate([qkv_weight.reshape(3 * share, width), out_weight, down_weight])
    in_parts = jnp.transpose(in_weight, (1, 0, 2))
    *arrived, weights = lax.optimization_barrier((*[pieces[mask] for mask in masks], weights))
    for mask, piece in zip(masks, arrived):
        pieces[mask], pieces[mask ^ 1] = piece, swap(piece, 1)
    out_pieces = gathered_by_mask(out_weight)
    taps = lax.dynamic_slice_in_dim(depth_weight, place * units, units, 3)
    scales = jnp.concatenate([taps.reshape(-1, units), attn_gain[None], mlp_gain[None]])
    mixed, cells = call(
        functools.partial(attend_body, count),
        [*pieces, weights],
        [((tokens, share), bf16), ((tokens, width), bf16)],
        flops=2 * tokens * width * 3 * share,
    )
    kept, sent, first = call(
        functools.partial(mlp_body, count, columns),
        [
            *gathered_by_mask(mixed),
            *out_pieces[1:],
            cells,
            weights,
            in_parts,
            scales,
        ],
        [((half, columns, width), f32)] + [((half, columns, width), bf16)] * 2,
        scratch=[((tokens + 2 * columns, units), f32)],
        flops=2 * tokens * width * (width + 3 * units),
        room=8,
    )
    total = kept + swap(sent, 1).astype(f32)
    far = [swap(total.astype(bf16), mask) for mask in range(3, count, 2)]
    step = rows // 2
    windows = call(
        functools.partial(norm_body, len(far), step),
        [total, first, scales, *far],
        [((step + 2, columns, width), bf16)] * count,
        scratch=[((half + 2, columns, width), bf16)],
        flops=8 * total.size,
    )
    windows = list(windows)
    for mask in range(1, count):
        pairs = [(i, (i + mask) % count) for i in range(count)]
        windows[mask] = lax.ppermute(windows[mask], "row", pairs)
    others = [swap(window, 1) for window in windows]
    hidden, own_part = call(
        functools.partial(first_conv_body, height),
        [*windows, *others, conv_first],
        [((count, rows + 2, columns, share), bf16), ((count, rows, columns, share), bf16)],
        scratch=[((count + 2, rows + 4, columns, width), bf16)],
        flops=2 * count * (rows + 2) * columns * 27 * width * share,
        room=8,
    )
    strip = columns // count
    pieces = gathered_by_mask(hidden)
    taps_shape = (count * rows * columns, 3 * share)
    field = ((count + 2, rows + 2, columns, 2 * share), bf16)
    flops = 2 * count * rows * columns * 27 * 2 * share * share
    (total,) = call(
        near_conv_body,
        [*pieces[:2], conv_second],
        [(taps_shape, f32)],
        scratch=[field],
        flops=flops,
        room=8,
    )
    strips = call(
        functools.partial(second_conv_body, count - 2),
        [*pieces[2:], total, own_part, conv_second],
        [((count * rows * strip, share), bf16)] * count,
        scratch=[field, ((count, rows, columns, share), f32)],
        flops=flops * (count // 2 - 1),
        room=8,
    )
    outs = list(strips)
    for mask in range(1, count):
        pairs = [(i, (i + mask) % count) for i in range(count)]
        outs[mask] = lax.ppermute(strips[mask], "frame", pairs)
    (decoded,) = call(join_body, outs, [((count, rows, strip, width), bf16)])
    return decoded


def solution(mesh):
    count = mesh.shape["frame"]
    square = mesh.shape["row"] == count > 1 and count & (count - 1) == 0
    body = by_frames if square else local
    in_specs = (
        P(("parts", "frame"), "row", None, None),
        P(None, "frame", None),
        P("frame", None),
        P(),
        P(None, None, "frame"),
        P(),
        P("frame", None),
        P(),
        P(None, None, None, "frame", None),
        P(None, None, None, "frame", None),
    )
    out_specs = P("parts", "row", "frame", None)
    return jax.shard_map(body, mesh=mesh, in_specs=in_specs, out_specs=out_specs, check_vma=False)
```
